32 devices in a mesh: parts: 2 (over x), lon: 16 (over z, y, core).
Axes of the slice: x: 2, y: 2, z: 4, core: 2. Of those that a mesh axis runs over, the one named last changes fastest.
Arguments:
- ocean_state: bfloat16 [64, 512, 256], P('parts', 'lon'), parts along dimension 0, may hold values from -6 to 6
- land_sea: int32 [32, 512], replicated, may hold values 0 or 1
- conv_weight: bfloat16 [3, 9, 256, 256], replicated, may hold values from -0.125 to 0.125
- up_weight: bfloat16 [3, 256, 1024], replicated, may hold values from -0.375 to 0.375
- down_weight: bfloat16 [3, 1024, 256], replicated, may hold values from -0.1875 to 0.1875
Outputs:
- next_state: bfloat16 [64, 512, 256], P('parts', 'lon'), parts along dimension 0
The draws below stay inside these ranges and needn't reach their ends.
There are 2 independent parts, one for each index of `parts`. The reference program is written for one: setup_inputs(seed, part) draws one part's arguments, and reference() takes and returns one part's arrays. A program takes and returns all parts, laid end to end along the dimension named above; an argument that names none is the same for every part. Nothing has to cross between parts.
All inputs are finite; a program needn't handle non-finite values.
Results may differ from the reference program's by a relative error of at most 0.009.
Values may be sent and summed in bfloat16 or wider, within the bound.
No kernel may reach another device: no remote copies, remote signals or barrier semaphores. Data moves between devices by JAX's collectives and lax.ppermute only.
A program may use at most 64 MiB of HBM per device.

```python
import jax
import jax.numpy as jnp
from jax import lax

C = 256
HID = 1024
LAYERS = 3
NLAT = 32
NLON = 512


def plant(drawn, rng, smallest, top_value):
    extent = drawn.shape
    index_at = [jax.random.randint(jax.random.fold_in(rng, axis), (), 0, extent[axis]) for axis in range(len(extent))]
    drawn = drawn.at[tuple(index_at)].set(smallest)
    longest = extent.index(max(extent))
    index_at[longest] = (index_at[longest] + 1) % extent[longest]
    return drawn.at[tuple(index_at)].set(top_value)


def levels(stream_key, dims, cuts, low, top_value):
    factor_of = 1.0
    for axis_at, parts in cuts:
        heights = jax.random.uniform(jax.random.fold_in(jax.random.fold_in(stream_key, 6), axis_at), (parts,), jnp.float32, low / len(cuts), top_value / len(cuts))
        factor_of = factor_of * jnp.repeat(jnp.exp(heights), dims[axis_at] // parts).reshape((-1,) + (1,) * (len(dims) - 1 - axis_at))
    return factor_of


def noise(own_key, extent, width, most, shards=(), dtype=jnp.bfloat16):
    level = levels(own_key, extent, shards, -0.22, 0.18) if shards else 1.0
    drawn = jax.random.normal(own_key, extent, jnp.float32) * width * level
    return jnp.minimum(jnp.maximum(drawn, -most), most).astype(dtype)


def setup_inputs(seed: int = 0, part: int = 0) -> dict:
    arg_keys = jax.random.split(jax.random.key(seed), 6)
    part_keys = jax.random.split(jax.random.fold_in(arg_keys[5], part), 6)
    return {
        "ocean_state": noise(part_keys[0], (NLAT, NLON, C), 1.0, 6.0, ((1, 16),)),
        "land_sea": plant((jax.random.randint(arg_keys[1], (NLAT, NLON), 0, 5) < 4).astype(jnp.int32), jax.random.fold_in(arg_keys[1], 1), 0, 1),
        "conv_weight": noise(arg_keys[2], (LAYERS, 9, C, C), (9 * C) ** -0.5, 0.125),
        "up_weight": noise(arg_keys[3], (LAYERS, C, HID), C ** -0.5, 0.375),
        "down_weight": noise(arg_keys[4], (LAYERS, HID, C), HID ** -0.5, 0.1875),
    }


def reference(ocean_state, land_sea, conv_weight, up_weight, down_weight):
    current = ocean_state
    mask_cells = land_sea.astype(jnp.float32).reshape(-1, 1)
    for layer in range(LAYERS):
        dilation = 2 ** (layer + 1)
        north = current[NLAT - dilation:][::-1, ::-1]
        south = jnp.zeros((dilation, NLON, C), jnp.bfloat16)
        extended = jnp.concatenate([south, current, north], axis=0)
        extended = jnp.concatenate([extended[:, NLON - dilation:], extended, extended[:, :dilation]], axis=1)
        total = jnp.zeros((NLAT * NLON, C), jnp.float32)
        for tap_row in range(3):
            for tap_col in range(3):
                window = extended[tap_row * dilation:tap_row * dilation + NLAT, tap_col * dilation:tap_col * dilation + NLON]
                total = total + jnp.dot(window.reshape(-1, C), conv_weight[layer, 3 * tap_row + tap_col], preferred_element_type=jnp.float32)
        mean_val = lax.optimization_barrier(jnp.mean(total, axis=-1, keepdims=True))
        centred = total - mean_val
        var_val = lax.optimization_barrier(jnp.mean(centred * centred, axis=-1, keepdims=True))
        normed = (centred * lax.rsqrt(var_val + 1e-05)).astype(jnp.bfloat16)
        hidden = jax.nn.gelu(jnp.dot(normed, up_weight[layer], preferred_element_type=jnp.float32), approximate=False).astype(jnp.bfloat16)
        branch = jnp.dot(hidden, down_weight[layer], preferred_element_type=jnp.float32)
        updated = mask_cells * (current.reshape(-1, C).astype(jnp.float32) + branch)
        current = updated.reshape(NLAT, NLON, C).astype(jnp.bfloat16)
    return current
```

```python
import functools

import jax
import jax.numpy as jnp
import numpy as np
from jax import lax
from jax.experimental import pallas as pl
from jax.experimental.pallas import tpu as pltpu
from jax.sharding import PartitionSpec as P

BF = jnp.bfloat16
F32 = jnp.float32
HALO = 16
DEEP = 14
RSQRT2 = np.float32(0.7071067811865476)


def conv_norm(layer, shifted, width, base, chunks, w_ref, nrm):
    dil = 2 ** (layer + 1)
    weight = w_ref[layer].reshape(-1, w_ref.shape[-1])
    at = 0
    for first, count, turned in chunks:
        taps = [(a, b) for a in range(3) for b in range(3)]
        if turned:
            taps = taps[::-1]
        size = count * width
        lhs = jnp.concatenate(
            [
                shifted[b, (first - base + (a - 1) * dil) * width : (first - base + (a - 1) * dil) * width + size]
                for a, b in taps
            ],
            axis=1,
        )
        conv = jnp.dot(lhs, weight, preferred_element_type=F32)
        mean = jnp.mean(conv, axis=-1, keepdims=True)
        centred = conv - mean
        var = jnp.mean(centred * centred, axis=-1, keepdims=True)
        nrm[at : at + size] = (centred * lax.rsqrt(var + 1e-05)).astype(BF)
        at += size


def mlp(layer, shifted, width, base, first, counts, up_ref, down_ref, mask_ref, nrm, store):
    at = 0
    row = first
    for count in counts:
        size = count * width
        pre = jnp.dot(nrm[at : at + size], up_ref[layer], preferred_element_type=F32)
        hidden = (0.5 * pre * (1.0 + lax.erf(pre * RSQRT2))).astype(BF)
        branch = jnp.dot(hidden, down_ref[layer], preferred_element_type=F32)
        centre = shifted[1, (row - base) * width : (row - base) * width + size].astype(F32)
        mask = mask_ref[row * width : row * width + size].astype(F32)
        mask = jnp.concatenate([mask, mask], axis=1)
        store(row, count, (mask * (centre + branch)).astype(BF))
        at += size
        row += count


def spread(shifted, width, at_row, values, start, dil):
    for b in range(3):
        lo = start + (b - 1) * dil
        shifted[b, at_row * width : (at_row + 1) * width] = values[lo : lo + width]


def spread_ref(shifted, width, at_row, ref, offset, start, dil):
    for b in range(3):
        lo = offset + start + (b - 1) * dil
        shifted[b, at_row * width : (at_row + 1) * width] = ref[lo : lo + width]


def south_kernel(
    left, own, right, m1, m2, m3, w, up, down, x1_tail, x2_tail, out, sh1, sh2, sh3, x1, x2, nrm
):
    for sh, rows, width in ((sh1, 2, 56), (sh2, 4, 48), (sh3, 8, 32)):
        for b in range(3):
            sh[b, : rows * width] = jnp.zeros((rows * width, 256), BF)
    for row in range(32):
        values = jnp.concatenate([left[row], own[row], right[row]], axis=0)
        spread(sh1, 56, row + 2, values, 4, 2)
    conv_norm(0, sh1, 56, -2, [(0, 8, False), (8, 8, False), (16, 8, False), (24, 6, False)], w, nrm)

    def store1(row, count, value):
        x1[row * 56 : (row + count) * 56] = value

    mlp(0, sh1, 56, -2, 0, [8, 8, 8, 6], up, down, m1, nrm, store1)
    x1_tail[...] = x1[22 * 56 : 30 * 56]
    for row in range(30):
        spread_ref(sh2, 48, row + 4, x1, row * 56, 4, 4)
    conv_norm(1, sh2, 48, -4, [(0, 10, False), (10, 8, False), (18, 8, False)], w, nrm)

    def store2(row, count, value):
        x2[row * 48 : (row + count) * 48] = value

    mlp(1, sh2, 48, -4, 0, [10, 8, 8], up, down, m2, nrm, store2)
    x2_tail[...] = x2[10 * 48 : 26 * 48]
    for row in range(26):
        spread_ref(sh3, 32, row + 8, x2, row * 48, 8, 8)
    conv_norm(2, sh3, 32, -8, [(0, 18, False)], w, nrm)

    def store3(row, count, value):
        out[row : row + count] = value.reshape(count, 32, 256)

    mlp(2, sh3, 32, -8, 0, [18], up, down, m3, nrm, store3)


def north_kernel(
    left, own, right, north, north_left, north_right, x1_tail, x2_tail, out_south,
    m1, m2, m3, w, up, down, out, sh1, sh2, sh3, x1, x2, nrm,
):
    out[0:18] = out_south[...]
    for row in range(4):
        values = jnp.concatenate([left[28 + row], own[28 + row], right[28 + row]], axis=0)
        spread(sh1, 56, row, values, 4, 2)
    for row in range(14):
        values = jnp.concatenate([north_left[row], north[row], north_right[row]], axis=0)
        spread(sh1, 56, row + 4, values, 4, 2)
    conv_norm(0, sh1, 56, 28, [(30, 2, False), (32, 12, True)], w, nrm)

    def store1(row, count, value):
        x1[(row - 30) * 56 : (row - 30 + count) * 56] = value

    mlp(0, sh1, 56, 28, 30, [8, 6], up, down, m1, nrm, store1)
    for row in range(8):
        spread_ref(sh2, 48, row, x1_tail, row * 56, 4, 4)
    for row in range(14):
        spread_ref(sh2, 48, row + 8, x1, row * 56, 4, 4)
    conv_norm(1, sh2, 48, 22, [(26, 6, False), (32, 8, True)], w, nrm)

    def store2(row, count, value):
        x2[(row - 26) * 48 : (row - 26 + count) * 48] = value

    mlp(1, sh2, 48, 22, 26, [14], up, down, m2, nrm, store2)
    for row in range(16):
        spread_ref(sh3, 32, row, x2_tail, row * 48, 8, 8)
    for row in range(14):
        spread_ref(sh3, 32, row + 16, x2, row * 48, 8, 8)
    conv_norm(2, sh3, 32, 10, [(18, 14, False)], w, nrm)

    def store3(row, count, value):
        out[row : row + count] = value.reshape(count, 32, 256)

    mlp(2, sh3, 32, 10, 18, [14], up, down, m3, nrm, store3)


def cost(cells):
    return pl.CostEstimate(
        flops=2 * cells * (9 * 256 * 256 + 2 * 256 * 1024), bytes_accessed=2**20, transcendentals=cells * 1024
    )


def call(kernel, name, outs, scratch_rows, cells, args):
    vmem = pl.BlockSpec(memory_space=pltpu.VMEM)
    r1, r2, r3, y1, y2, normed = scratch_rows
    return pl.pallas_call(
        kernel,
        name=name,
        out_shape=tuple(jax.ShapeDtypeStruct(shape, BF) for shape in outs),
        in_specs=[vmem] * len(args),
        out_specs=tuple(vmem for _ in outs),
        scratch_shapes=[
            pltpu.VMEM((3, r1 * 56, 256), BF),
            pltpu.VMEM((3, r2 * 48, 256), BF),
            pltpu.VMEM((3, r3 * 32, 256), BF),
            pltpu.VMEM((y1 * 56, 256), BF),
            pltpu.VMEM((y2 * 48, 256), BF),
            pltpu.VMEM((normed, 256), BF),
        ],
        compiler_params=pltpu.CompilerParams(vmem_limit_bytes=24 * 2**20),
        cost_estimate=cost(cells),
    )(*args)


def around(value, step):
    count = lax.axis_size("lon")
    return lax.ppermute(value, "lon", [(i, (i + step) % count) for i in range(count)])


def per_device(own, land_sea, w, up, down):
    count = lax.axis_size("lon")
    cols = own.shape[1]
    left = around(own[:, cols - HALO :], 1)
    right = around(own[:, :HALO], -1)
    strip = own[own.shape[0] - DEEP :][::-1, ::-1]
    north = lax.ppermute(strip, "lon", [(i, count - 1 - i) for i in range(count)])

    land = jnp.concatenate([land_sea, land_sea[::-1, ::-1][:DEEP]], axis=0).astype(BF)
    land = jnp.concatenate([land[:, -HALO:], land, land[:, :HALO]], axis=1)
    land = lax.dynamic_slice_in_dim(land, lax.axis_index("lon") * cols, cols + 2 * HALO, 1)

    def cells_mask(rows, margin):
        part = land[:rows, HALO - margin : HALO + cols + margin].reshape(-1, 1)
        return jnp.broadcast_to(part, (part.shape[0], 128))

    masks = (cells_mask(44, 12), cells_mask(40, 8), cells_mask(32, 0))
    weights = (w, up, down)
    x1_tail, x2_tail, out_south = call(
        south_kernel, "south", [(8 * 56, 256), (16 * 48, 256), (18, 32, 256)],
        (34, 34, 34, 30, 26, 30 * 56), 3504, (left, own, right, *masks, *weights),
    )
    north, x1_tail = lax.optimization_barrier((north, x1_tail))
    north_left = around(north[:, cols - HALO :], 1)
    north_right = around(north[:, :HALO], -1)
    (out,) = call(
        north_kernel, "north", [(32, 32, 256)], (18, 22, 30, 14, 14, 14 * 56), 1904,
        (left, own, right, north, north_left, north_right, x1_tail, x2_tail, out_south, *masks, *weights),
    )
    return out


def solution(mesh):
    in_specs = (P("parts", "lon", None), P(), P(), P(), P())
    out_specs = P("parts", "lon", None)
    return jax.shard_map(
        per_device, mesh=mesh, in_specs=in_specs, out_specs=out_specs, check_vma=False
    )
```

```python
import functools

import jax
import jax.numpy as jnp
import numpy as np
from jax import lax
from jax.experimental import pallas as pl
from jax.experimental.pallas import tpu as pltpu
from jax.sharding import PartitionSpec as P

BF = jnp.bfloat16
F32 = jnp.float32
HALO = 16
DEEP = 14
LIMIT = 24
RSQRT2 = np.float32(0.7071067811865476)


def conv_norm(layer, shifted, width, base, chunks, w_ref, nrm):
    dil = 2 ** (layer + 1)
    weight = w_ref[layer].reshape(-1, w_ref.shape[-1])
    at = 0
    for first, count, turned in chunks:
        taps = [(a, b) for a in range(3) for b in range(3)]
        if turned:
            taps = taps[::-1]
        size = count * width
        lhs = jnp.concatenate(
            [
                shifted[b, (first - base + (a - 1) * dil) * width : (first - base + (a - 1) * dil) * width + size]
                for a, b in taps
            ],
            axis=1,
        )
        conv = jnp.dot(lhs, weight, preferred_element_type=F32)
        mean = jnp.mean(conv, axis=-1, keepdims=True)
        centred = conv - mean
        var = jnp.mean(centred * centred, axis=-1, keepdims=True)
        nrm[at : at + size] = (centred * lax.rsqrt(var + 1e-05)).astype(BF)
        at += size


def mlp(layer, shifted, width, base, first, counts, up_ref, down_ref, mask_ref, nrm, store, mask_base=0):
    at = 0
    row = first
    for count in counts:
        size = count * width
        pre = jnp.dot(nrm[at : at + size], up_ref[layer], preferred_element_type=F32)
        hidden = (0.5 * pre * (1.0 + lax.erf(pre * RSQRT2))).astype(BF)
        branch = jnp.dot(hidden, down_ref[layer], preferred_element_type=F32)
        centre = shifted[1, (row - base) * width : (row - base) * width + size].astype(F32)
        mask = mask_ref[(row - mask_base) * width : (row - mask_base) * width + size].astype(F32)
        mask = jnp.concatenate([mask, mask], axis=1)
        store(row, count, (mask * (centre + branch)).astype(BF))
        at += size
        row += count


def spread(shifted, at, values, starts, size, dil):
    for b in range(3):
        for k, start in enumerate(starts):
            lo = start + (b - 1) * dil
            shifted[b, at + k * size : at + (k + 1) * size] = values[lo : lo + size]


def clear(shifted, size):
    for b in range(3):
        shifted[b, :size] = jnp.zeros((size, shifted.shape[-1]), BF)


def keep(ref, width, base):
    def store(row, count, value):
        ref[(row - base) * width : (row - base + count) * width] = value

    return store


def wide(row, left, own, right):
    return jnp.concatenate([left[row], own[row], right[row]], axis=0)


def inner_kernel(own, mask, w, up, down, x1, x2, sh1, sh2, nrm):
    clear(sh1, 2 * 32)
    clear(sh2, 4 * 32)
    edge = jnp.zeros((HALO, own.shape[-1]), BF)
    for row in range(32):
        spread(sh1, (row + 2) * 32, jnp.concatenate([edge, own[row], edge], axis=0), [16], 32, 2)
    conv_norm(0, sh1, 32, -2, [(0, 15, False), (15, 15, False)], w, nrm)
    mlp(0, sh1, 32, -2, 0, [15, 15], up, down, mask, nrm, keep(x1, 32, 0))
    for row in range(30):
        values = jnp.concatenate([edge, x1[row * 32 : (row + 1) * 32], edge], axis=0)
        spread(sh2, (row + 4) * 32, values, [16], 32, 4)
    conv_norm(1, sh2, 32, -4, [(0, 13, False), (13, 13, False)], w, nrm)
    mlp(1, sh2, 32, -4, 0, [13, 13], up, down, mask, nrm, keep(x2, 32, 0))


def south_kernel(
    left, own, right, x1_mid, x2_mid, e1, e2, mask, w, up, down,
    x1_tail, x2_tail, out, sh1, sh2, sh3, x1, x2, nrm,
):
    clear(sh1, 2 * 32)
    clear(sh2, 4 * 32)
    clear(sh3, 8 * 32)
    for row in range(32):
        spread(sh1, (row + 2) * 32, wide(row, left, own, right), [4, 44], 16, 2)
    conv_norm(0, sh1, 32, -2, [(0, 15, False), (15, 15, False)], w, nrm)
    mlp(0, sh1, 32, -2, 0, [15, 15], up, down, e1, nrm, keep(x1, 32, 0))

    def row1(row):
        at = row * 32
        return jnp.concatenate([x1[at : at + 16], x1_mid[at + 4 : at + 28], x1[at + 16 : at + 32]], axis=0)

    for row in range(30):
        values = row1(row)
        if row >= 22:
            x1_tail[(row - 22) * 56 : (row - 21) * 56] = values
        spread(sh2, (row + 4) * 32, values, [4, 36], 16, 4)
    conv_norm(1, sh2, 32, -4, [(0, 13, False), (13, 13, False)], w, nrm)
    mlp(1, sh2, 32, -4, 0, [13, 13], up, down, e2, nrm, keep(x2, 32, 0))
    for row in range(26):
        at = row * 32
        values = jnp.concatenate([x2[at : at + 16], x2_mid[at + 8 : at + 24], x2[at + 16 : at + 32]], axis=0)
        if row >= 10:
            x2_tail[(row - 10) * 48 : (row - 9) * 48] = values
        spread(sh3, (row + 8) * 32, values, [8], 32, 8)
    conv_norm(2, sh3, 32, -8, [(0, 9, False), (9, 9, False)], w, nrm)

    def store3(row, count, value):
        out[row : row + count] = value.reshape(count, 32, 256)

    mlp(2, sh3, 32, -8, 0, [9, 9], up, down, mask, nrm, store3)


def north_kernel(
    left, own, right, north, north_left, north_right, x1_tail, x2_tail, out_south,
    m1, m2, mask, w, up, down, out, sh1, sh2, sh3, x1, x2, nrm, last, sems,
):
    first = pltpu.make_async_copy(out_south, out.at[0:18], sems.at[0])
    first.start()
    for row in range(4):
        spread(sh1, row * 56, wide(28 + row, left, own, right), [4], 56, 2)
    for row in range(14):
        spread(sh1, (row + 4) * 56, wide(row, north_left, north, north_right), [4], 56, 2)
    conv_norm(0, sh1, 56, 28, [(30, 2, False), (32, 6, True), (38, 6, True)], w, nrm)
    mlp(0, sh1, 56, 28, 30, [8, 6], up, down, m1, nrm, keep(x1, 56, 30), 30)
    for row in range(8):
        spread(sh2, row * 48, x1_tail[row * 56 : (row + 1) * 56], [4], 48, 4)
    for row in range(14):
        spread(sh2, (row + 8) * 48, x1[row * 56 : (row + 1) * 56], [4], 48, 4)
    conv_norm(1, sh2, 48, 22, [(26, 6, False), (32, 8, True)], w, nrm)
    mlp(1, sh2, 48, 22, 26, [7, 7], up, down, m2, nrm, keep(x2, 48, 26), 26)
    for row in range(16):
        spread(sh3, row * 32, x2_tail[row * 48 : (row + 1) * 48], [8], 32, 8)
    for row in range(14):
        spread(sh3, (row + 16) * 32, x2[row * 48 : (row + 1) * 48], [8], 32, 8)
    conv_norm(2, sh3, 32, 10, [(18, 7, False), (25, 7, False)], w, nrm)

    def store3(row, count, value):
        last[row - 18 : row - 18 + count] = value.reshape(count, 32, 256)

    mlp(2, sh3, 32, 10, 18, [7, 7], up, down, mask, nrm, store3)
    second = pltpu.make_async_copy(last, out.at[18:32], sems.at[1])
    second.start()
    first.wait()
    second.wait()


def cost(cells):
    return pl.CostEstimate(
        flops=2 * cells * (9 * 256 * 256 + 2 * 256 * 1024), bytes_accessed=2**20, transcendentals=cells * 1024
    )


VMEM = pl.BlockSpec(memory_space=pltpu.VMEM)
HBM = pl.BlockSpec(memory_space=pltpu.HBM)


def call(kernel, name, outs, in_specs, out_specs, scratch, cells, args):
    return pl.pallas_call(
        kernel,
        name=name,
        out_shape=tuple(jax.ShapeDtypeStruct(shape, BF) for shape in outs),
        in_specs=in_specs,
        out_specs=tuple(out_specs),
        scratch_shapes=scratch,
        compiler_params=pltpu.CompilerParams(vmem_limit_bytes=LIMIT * 2**20),
        cost_estimate=cost(cells),
    )(*args)


def taps(rows, width):
    return pltpu.VMEM((3, rows * width, 256), BF)


def flat(rows, width):
    return pltpu.VMEM((rows * width, 256), BF)


def inner_call(own, mask, w, up, down):
    return call(
        inner_kernel, "inner", [(30 * 32, 256), (26 * 32, 256)],
        [VMEM] * 5, [VMEM] * 2,
        [taps(34, 32), taps(34, 32), flat(30, 32)],
        1792, (own, mask, w, up, down),
    )


def south_call(*args):
    return call(
        south_kernel, "south", [(8 * 56, 256), (16 * 48, 256), (18, 32, 256)], [VMEM] * len(args), [VMEM] * 3,
        [taps(34, 32), taps(34, 32), taps(34, 32), flat(30, 32), flat(26, 32), flat(30, 32)],
        2368, args,
    )


def north_call(*args):
    (out,) = call(
        north_kernel, "north", [(32, 32, 256)], [VMEM] * len(args), [HBM],
        [
            taps(18, 56), taps(22, 48), taps(30, 32), flat(14, 56), flat(14, 48), flat(14, 56),
            pltpu.VMEM((14, 32, 256), BF), pltpu.SemaphoreType.DMA((2,)),
        ],
        1904, args,
    )
    return out


def around(value, step):
    count = lax.axis_size("lon")
    return lax.ppermute(value, "lon", [(i, (i + step) % count) for i in range(count)])


def per_device(own, land_sea, w, up, down):
    count = lax.axis_size("lon")
    cols = own.shape[1]
    left = around(own[:, cols - HALO :], 1)
    right = around(own[:, :HALO], -1)
    strip = own[own.shape[0] - DEEP :][::-1, ::-1]
    north = lax.ppermute(strip, "lon", [(i, count - 1 - i) for i in range(count)])

    def cells_mask(parts):
        part = jnp.concatenate(parts, axis=1) if len(parts) > 1 else parts[0]
        part = part.reshape(-1, 1)
        return jnp.broadcast_to(part, (part.shape[0], 128))

    land_sea = land_sea.astype(BF)
    at = lax.axis_index("lon") * cols
    mask = cells_mask([lax.dynamic_slice_in_dim(land_sea, at, cols, 1)])
    weights = (w, up, down)
    x1_mid, x2_mid = inner_call(own, mask, w, up, down)

    land = jnp.concatenate([land_sea, land_sea[::-1, ::-1][:DEEP]], axis=0)
    land = jnp.concatenate([land[:, -HALO:], land, land[:, :HALO]], axis=1)
    land = lax.dynamic_slice_in_dim(land, at, cols + 2 * HALO, 1)
    e1 = cells_mask([land[:30, 4:20], land[:30, 44:60]])
    e2 = cells_mask([land[:26, 8:24], land[:26, 40:56]])
    m1 = cells_mask([land[30:44, 4:60]])
    m2 = cells_mask([land[26:40, 8:56]])
    left, right, m1, m2 = lax.optimization_barrier((left, right, m1, m2))
    x1_tail, x2_tail, out_south = south_call(left, own, right, x1_mid, x2_mid, e1, e2, mask, *weights)
    north, x1_tail = lax.optimization_barrier((north, x1_tail))
    north_left = around(north[:, cols - HALO :], 1)
    north_right = around(north[:, :HALO], -1)
    return north_call(
        left, own, right, north, north_left, north_right, x1_tail, x2_tail, out_south, m1, m2, mask, *weights
    )


def solution(mesh):
    in_specs = (P("parts", "lon", None), P(), P(), P(), P())
    out_specs = P("parts", "lon", None)
    return jax.shard_map(
        per_device, mesh=mesh, in_specs=in_specs, out_specs=out_specs, check_vma=False
    )
```

```python
import functools

import jax
import jax.numpy as jnp
import numpy as np
from jax import lax
from jax.experimental import pallas as pl
from jax.experimental.pallas import tpu as pltpu
from jax.sharding import PartitionSpec as P

BF = jnp.bfloat16
F32 = jnp.float32
HALO = 16
DEEP = 14
LIMIT = 51
RSQRT2 = np.float32(0.7071067811865476)


def conv_norm(layer, shifted, width, base, chunks, w_ref, nrm):
    dil = 2 ** (layer + 1)
    weight = w_ref[layer].reshape(-1, w_ref.shape[-1])
    at = 0
    for first, count, turned in chunks:
        taps = [(a, b) for a in range(3) for b in range(3)]
        if turned:
            taps = taps[::-1]
        size = count * width
        lhs = jnp.concatenate(
            [
                shifted[b, (first - base + (a - 1) * dil) * width : (first - base + (a - 1) * dil) * width + size]
                for a, b in taps
            ],
            axis=1,
        )
        conv = jnp.dot(lhs, weight, preferred_element_type=F32)
        mean = jnp.mean(conv, axis=-1, keepdims=True)
        centred = conv - mean
        var = jnp.mean(centred * centred, axis=-1, keepdims=True)
        nrm[at : at + size] = (centred * lax.rsqrt(var + 1e-05)).astype(BF)
        at += size


def mlp(layer, shifted, width, base, first, counts, up_ref, down_ref, mask_ref, nrm, store, mask_base=0):
    at = 0
    row = first
    for count in counts:
        size = count * width
        pre = jnp.dot(nrm[at : at + size], up_ref[layer], preferred_element_type=F32)
        hidden = (0.5 * pre * (1.0 + lax.erf(pre * RSQRT2))).astype(BF)
        branch = jnp.dot(hidden, down_ref[layer], preferred_element_type=F32)
        centre = shifted[1, (row - base) * width : (row - base) * width + size].astype(F32)
        mask = mask_ref[(row - mask_base) * width : (row - mask_base) * width + size].astype(F32)
        mask = jnp.concatenate([mask, mask], axis=1)
        store(row, count, (mask * (centre + branch)).astype(BF))
        at += size
        row += count


def spread(shifted, at, values, starts, size, dil):
    for b in range(3):
        for k, start in enumerate(starts):
            lo = start + (b - 1) * dil
            shifted[b, at + k * size : at + (k + 1) * size] = values[lo : lo + size]


def clear(shifted, size):
    for b in range(3):
        shifted[b, :size] = jnp.zeros((size, shifted.shape[-1]), BF)


def keep(ref, width, base):
    def store(row, count, value):
        ref[(row - base) * width : (row - base + count) * width] = value

    return store


def fetch(layers, sources, targets, sems):
    copies = [
        [pltpu.make_async_copy(src.at[layer], dst.at[layer], sems.at[k, layer]) for k, (src, dst) in enumerate(zip(sources, targets))]
        for layer in range(layers)
    ]
    for group in copies:
        for copy in group:
            copy.start()

    def arrived(layer, *which):
        for k in which:
            copies[layer][k].wait()

    return arrived


def diagonal(turned):
    rows = lax.broadcasted_iota(jnp.int32, (64, 64), 0)
    cols = lax.broadcasted_iota(jnp.int32, (64, 64), 1)
    return rows + cols == 63 if turned else rows == cols


def spread_mask(land, row, turned):
    line = jnp.where(diagonal(turned), land[row : row + 1], 0.0).astype(BF)
    return jnp.dot(line, jnp.ones((64, 128), BF), preferred_element_type=F32).astype(BF)


def wide(row, left, own, right):
    return jnp.concatenate([left[row], own[row], right[row]], axis=0)


def inner_kernel(own, land, w_hbm, up_hbm, down_hbm, x1, x2, mask, w, up, down, sems, sh1, sh2, nrm):
    arrived = fetch(2, (w_hbm, up_hbm, down_hbm), (w, up, down), sems)
    clear(sh1, 2 * 32)
    clear(sh2, 4 * 32)
    edge = jnp.zeros((HALO, own.shape[-1]), BF)
    for row in range(32):
        spread(sh1, (row + 2) * 32, jnp.concatenate([edge, own[row], edge], axis=0), [16], 32, 2)
        mask[row * 32 : (row + 1) * 32] = spread_mask(land, row, False)[16:48]
    arrived(0, 0)
    conv_norm(0, sh1, 32, -2, [(0, 15, False), (15, 15, False)], w, nrm)
    arrived(0, 1, 2)
    mlp(0, sh1, 32, -2, 0, [15, 15], up, down, mask, nrm, keep(x1, 32, 0))
    for row in range(30):
        values = jnp.concatenate([edge, x1[row * 32 : (row + 1) * 32], edge], axis=0)
        spread(sh2, (row + 4) * 32, values, [16], 32, 4)
    arrived(1, 0, 1, 2)
    conv_norm(1, sh2, 32, -4, [(0, 13, False), (13, 13, False)], w, nrm)
    mlp(1, sh2, 32, -4, 0, [13, 13], up, down, mask, nrm, keep(x2, 32, 0))


def south_kernel(
    left, own, right, x1_mid, x2_mid, land, mask, w_hbm, up_hbm, down_hbm,
    x1_tail, x2_tail, out, w, up, down, sems, sh1, sh2, sh3, x1, x2, nrm, e1, e2,
):
    arrived = fetch(3, (w_hbm, up_hbm, down_hbm), (w, up, down), sems)
    clear(sh1, 2 * 32)
    clear(sh2, 4 * 32)
    clear(sh3, 8 * 32)
    for row in range(32):
        spread(sh1, (row + 2) * 32, wide(row, left, own, right), [4, 44], 16, 2)
    for row in range(30):
        cells = spread_mask(land, row, False)
        e1[row * 32 : (row + 1) * 32] = jnp.concatenate([cells[4:20], cells[44:60]], axis=0)
        if row < 26:
            e2[row * 32 : (row + 1) * 32] = jnp.concatenate([cells[8:24], cells[40:56]], axis=0)
    arrived(0, 0)
    conv_norm(0, sh1, 32, -2, [(0, 15, False), (15, 15, False)], w, nrm)
    arrived(0, 1, 2)
    mlp(0, sh1, 32, -2, 0, [15, 15], up, down, e1, nrm, keep(x1, 32, 0))

    def row1(row):
        at = row * 32
        return jnp.concatenate([x1[at : at + 16], x1_mid[at + 4 : at + 28], x1[at + 16 : at + 32]], axis=0)

    for row in range(30):
        values = row1(row)
        if row >= 22:
            x1_tail[(row - 22) * 56 : (row - 21) * 56] = values
        spread(sh2, (row + 4) * 32, values, [4, 36], 16, 4)
    arrived(1, 0)
    conv_norm(1, sh2, 32, -4, [(0, 13, False), (13, 13, False)], w, nrm)
    arrived(1, 1, 2)
    mlp(1, sh2, 32, -4, 0, [13, 13], up, down, e2, nrm, keep(x2, 32, 0))
    for row in range(26):
        at = row * 32
        values = jnp.concatenate([x2[at : at + 16], x2_mid[at + 8 : at + 24], x2[at + 16 : at + 32]], axis=0)
        if row >= 10:
            x2_tail[(row - 10) * 48 : (row - 9) * 48] = values
        spread(sh3, (row + 8) * 32, values, [8], 32, 8)
    arrived(2, 0)
    conv_norm(2, sh3, 32, -8, [(0, 9, False), (9, 9, False)], w, nrm)

    def store3(row, count, value):
        out[row : row + count] = value.reshape(count, 32, 256)

    arrived(2, 1, 2)
    mlp(2, sh3, 32, -8, 0, [9, 9], up, down, mask, nrm, store3)


def north_kernel(
    left, own, right, north, north_left, north_right, x1_tail, x2_tail, out_south,
    land, land_north, mask, w_hbm, up_hbm, down_hbm, out, w, up, down, w_sems, sh1, sh2, sh3, x1, x2, nrm, last, sems, m1, m2,
):
    arrived = fetch(3, (w_hbm, up_hbm, down_hbm), (w, up, down), w_sems)
    first = pltpu.make_async_copy(out_south, out.at[0:18], sems.at[0])
    first.start()
    turn = jnp.where(diagonal(True), 1.0, 0.0).astype(BF)
    for row in range(4):
        spread(sh1, row * 56, wide(28 + row, left, own, right), [4], 56, 2)
    for row in range(14):
        source = wide(13 - row, north_right, north, north_left)
        turned = jnp.dot(turn, source, preferred_element_type=F32).astype(BF)
        spread(sh1, (row + 4) * 56, turned, [4], 56, 2)
    for row in range(26, 44):
        cells = spread_mask(land, row, False) if row < 32 else spread_mask(land_north, 45 - row, True)
        if row >= 30:
            m1[(row - 30) * 56 : (row - 29) * 56] = cells[4:60]
        if row < 40:
            m2[(row - 26) * 48 : (row - 25) * 48] = cells[8:56]
    arrived(0, 0)
    conv_norm(0, sh1, 56, 28, [(30, 2, False), (32, 6, True), (38, 6, True)], w, nrm)
    arrived(0, 1, 2)
    mlp(0, sh1, 56, 28, 30, [8, 6], up, down, m1, nrm, keep(x1, 56, 30), 30)
    for row in range(8):
        spread(sh2, row * 48, x1_tail[row * 56 : (row + 1) * 56], [4], 48, 4)
    for row in range(14):
        spread(sh2, (row + 8) * 48, x1[row * 56 : (row + 1) * 56], [4], 48, 4)
    arrived(1, 0)
    conv_norm(1, sh2, 48, 22, [(26, 6, False), (32, 8, True)], w, nrm)
    arrived(1, 1, 2)
    mlp(1, sh2, 48, 22, 26, [7, 7], up, down, m2, nrm, keep(x2, 48, 26), 26)
    for row in range(16):
        spread(sh3, row * 32, x2_tail[row * 48 : (row + 1) * 48], [8], 32, 8)
    for row in range(14):
        spread(sh3, (row + 16) * 32, x2[row * 48 : (row + 1) * 48], [8], 32, 8)
    arrived(2, 0)
    conv_norm(2, sh3, 32, 10, [(18, 7, False), (25, 7, False)], w, nrm)

    def store3(row, count, value):
        last[row - 18 : row - 18 + count] = value.reshape(count, 32, 256)

    arrived(2, 1, 2)
    mlp(2, sh3, 32, 10, 18, [7, 7], up, down, mask, nrm, store3)
    second = pltpu.make_async_copy(last, out.at[18:32], sems.at[1])
    second.start()
    first.wait()
    second.wait()


def cost(cells):
    return pl.CostEstimate(
        flops=2 * cells * (9 * 256 * 256 + 2 * 256 * 1024), bytes_accessed=2**20, transcendentals=cells * 1024
    )


VMEM = pl.BlockSpec(memory_space=pltpu.VMEM)
HBM = pl.BlockSpec(memory_space=pltpu.HBM)


def call(kernel, name, outs, in_specs, out_specs, scratch, cells, args):
    return pl.pallas_call(
        kernel,
        name=name,
        out_shape=tuple(jax.ShapeDtypeStruct(shape, BF) for shape in outs),
        in_specs=in_specs,
        out_specs=tuple(out_specs),
        scratch_shapes=scratch,
        compiler_params=pltpu.CompilerParams(vmem_limit_bytes=LIMIT * 2**20),
        cost_estimate=cost(cells),
    )(*args)


def taps(rows, width):
    return pltpu.VMEM((3, rows * width, 256), BF)


def flat(rows, width):
    return pltpu.VMEM((rows * width, 256), BF)


def weight_scratch(layers, *weights):
    return [pltpu.VMEM((layers, *value.shape[1:]), BF) for value in weights] + [pltpu.SemaphoreType.DMA((3, layers))]


def inner_call(own, land, w, up, down):
    return call(
        inner_kernel, "inner", [(30 * 32, 256), (26 * 32, 256), (32 * 32, 128)],
        [VMEM] * 2 + [HBM] * 3, [VMEM] * 3,
        weight_scratch(2, w, up, down) + [taps(34, 32), taps(34, 32), flat(30, 32)],
        1792, (own, land, w, up, down),
    )


def south_call(*args):
    return call(
        south_kernel, "south", [(8 * 56, 256), (16 * 48, 256), (18, 32, 256)], [VMEM] * (len(args) - 3) + [HBM] * 3, [VMEM] * 3,
        weight_scratch(3, *args[-3:]) + [taps(34, 32), taps(34, 32), taps(34, 32), flat(30, 32), flat(26, 32), flat(30, 32),
         pltpu.VMEM((30 * 32, 128), BF), pltpu.VMEM((26 * 32, 128), BF)],
        2368, args,
    )


def north_call(*args):
    (out,) = call(
        north_kernel, "north", [(32, 32, 256)], [VMEM] * (len(args) - 3) + [HBM] * 3, [HBM],
        weight_scratch(3, *args[-3:]) + [
            taps(18, 56), taps(22, 48), taps(30, 32), flat(14, 56), flat(14, 48), flat(14, 56),
            pltpu.VMEM((14, 32, 256), BF), pltpu.SemaphoreType.DMA((2,)),
            pltpu.VMEM((14 * 56, 128), BF), pltpu.VMEM((14 * 48, 128), BF),
        ],
        1904, args,
    )
    return out


def around(value, step):
    count = lax.axis_size("lon")
    return lax.ppermute(value, "lon", [(i, (i + step) % count) for i in range(count)])


def per_device(own, land_sea, w, up, down):
    count = lax.axis_size("lon")
    cols = own.shape[1]
    left = around(own[:, cols - HALO :], 1)
    right = around(own[:, :HALO], -1)
    north = lax.ppermute(own[own.shape[0] - DEEP :], "lon", [(i, count - 1 - i) for i in range(count)])

    at = lax.axis_index("lon")
    land = jnp.concatenate([land_sea[:, -HALO:], land_sea, land_sea[:, :HALO]], axis=1).astype(F32)
    land_north = lax.dynamic_slice_in_dim(land[-DEEP:], (count - 1 - at) * cols, cols + 2 * HALO, 1)
    land = lax.dynamic_slice_in_dim(land, at * cols, cols + 2 * HALO, 1)
    weights = (w, up, down)
    x1_mid, x2_mid, mask = inner_call(own, land, *weights)
    left, right, land_north = lax.optimization_barrier((left, right, land_north))
    x1_tail, x2_tail, out_south = south_call(left, own, right, x1_mid, x2_mid, land, mask, *weights)
    north, x1_tail = lax.optimization_barrier((north, x1_tail))
    north_left = around(north[:, :HALO], 1)
    north_right = around(north[:, cols - HALO :], -1)
    return north_call(
        left, own, right, north, north_left, north_right, x1_tail, x2_tail, out_south, land, land_north, mask, *weights
    )


def solution(mesh):
    in_specs = (P("parts", "lon", None), P(), P(), P(), P())
    out_specs = P("parts", "lon", None)
    return jax.shard_map(
        per_device, mesh=mesh, in_specs=in_specs, out_specs=out_specs, check_vma=False
    )
```

```python
import functools

import jax
import jax.numpy as jnp
import numpy as np
from jax import lax
from jax.experimental import pallas as pl
from jax.experimental.pallas import tpu as pltpu
from jax.sharding import PartitionSpec as P

BF = jnp.bfloat16
F32 = jnp.float32
HALO = 16
DEEP = 14
LIMIT = 20
EDGE_CELLS = 2048
RSQRT2 = np.float32(0.7071067811865476)


def conv_norm(layer, shifted, width, base, chunks, w_ref, nrm):
    dil = 2 ** (layer + 1)
    weight = w_ref[layer].reshape(-1, w_ref.shape[-1])
    at = 0
    for first, count, turned in chunks:
        taps = [(a, b) for a in range(3) for b in range(3)]
        if turned:
            taps = taps[::-1]
        size = count * width
        lhs = jnp.concatenate(
            [
                shifted[b, (first - base + (a - 1) * dil) * width : (first - base + (a - 1) * dil) * width + size]
                for a, b in taps
            ],
            axis=1,
        )
        conv = jnp.dot(lhs, weight, preferred_element_type=F32)
        mean = jnp.mean(conv, axis=-1, keepdims=True)
        centred = conv - mean
        var = jnp.mean(centred * centred, axis=-1, keepdims=True)
        nrm[at : at + size] = (centred * lax.rsqrt(var + 1e-05)).astype(BF)
        at += size


def mlp(layer, shifted, width, base, first, counts, up_ref, down_ref, mask_ref, nrm, store, mask_base=0):
    at = 0
    row = first
    for count in counts:
        size = count * width
        pre = jnp.dot(nrm[at : at + size], up_ref[layer], preferred_element_type=F32)
        hidden = (0.5 * pre * (1.0 + lax.erf(pre * RSQRT2))).astype(BF)
        branch = jnp.dot(hidden, down_ref[layer], preferred_element_type=F32)
        centre = shifted[1, (row - base) * width : (row - base) * width + size].astype(F32)
        mask = mask_ref[(row - mask_base) * width : (row - mask_base) * width + size].astype(F32)
        mask = jnp.concatenate([mask, mask], axis=1)
        store(row, count, (mask * (centre + branch)).astype(BF))
        at += size
        row += count


def spread(shifted, at, values, starts, size, dil):
    for b in range(3):
        for k, start in enumerate(starts):
            lo = start + (b - 1) * dil
            shifted[b, at + k * size : at + (k + 1) * size] = values[lo : lo + size]


def clear(shifted, size):
    for b in range(3):
        shifted[b, :size] = jnp.zeros((size, shifted.shape[-1]), BF)


def keep(ref, width, base):
    def store(row, count, value):
        ref[(row - base) * width : (row - base + count) * width] = value

    return store


def diagonal(turned):
    rows = lax.broadcasted_iota(jnp.int32, (64, 64), 0)
    cols = lax.broadcasted_iota(jnp.int32, (64, 64), 1)
    return rows + cols == 63 if turned else rows == cols


def spread_mask(land, first, count, turned):
    lines = jnp.where(diagonal(turned)[None], land[first : first + count][:, None, :], 0.0).astype(BF)
    cells = jnp.dot(lines.reshape(count * 64, 64), jnp.ones((64, 128), BF), preferred_element_type=F32)
    return cells.astype(BF).reshape(count, 64, 128)


def window(whole, first):
    total = whole.shape[1]
    source = lax.broadcasted_iota(jnp.int32, (total, 64), 0)
    target = lax.broadcasted_iota(jnp.int32, (total, 64), 1) + first
    target = jnp.where(target < 0, target + total, target)
    target = jnp.where(target >= total, target - total, target)
    pick = jnp.where(source == target, 1.0, 0.0).astype(BF)
    return jnp.dot(whole, pick, preferred_element_type=F32)


def edges_kernel(own, left, right, top, sems):
    copies = [
        pltpu.make_async_copy(own.at[:, 0:HALO], left, sems.at[0]),
        pltpu.make_async_copy(own.at[:, 32 - HALO : 32], right, sems.at[1]),
        pltpu.make_async_copy(own.at[32 - DEEP : 32], top, sems.at[2]),
    ]
    for copy in copies:
        copy.start()
    for copy in copies:
        copy.wait()


def wide(row, left, own, right):
    return jnp.concatenate([left[row], own[row], right[row]], axis=0)


def first_kernel(own, land_sea, w, up, down, x1, mask, land, land_north, sh1, nrm):
    me = lax.axis_index("lon")
    whole = land_sea[...].astype(F32).astype(BF)
    land[...] = window(whole, me * 32 - HALO)
    land_north[...] = window(whole, (lax.axis_size("lon") - 1 - me) * 32 - HALO)[32 - DEEP :]
    mask[...] = spread_mask(land, 0, 32, False)[:, 16:48].reshape(32 * 32, 128)
    clear(sh1, 2 * 32)
    edge = jnp.zeros((HALO, own.shape[-1]), BF)
    for row in range(32):
        spread(sh1, (row + 2) * 32, jnp.concatenate([edge, own[row], edge], axis=0), [16], 32, 2)
    conv_norm(0, sh1, 32, -2, [(0, 15, False), (15, 15, False)], w, nrm)
    mlp(0, sh1, 32, -2, 0, [15, 15], up, down, mask, nrm, keep(x1, 32, 0))


def second_kernel(x1, mask, w, up, down, x2, sh2, nrm):
    clear(sh2, 4 * 32)
    edge = jnp.zeros((HALO, x1.shape[-1]), BF)
    for row in range(30):
        values = jnp.concatenate([edge, x1[row * 32 : (row + 1) * 32], edge], axis=0)
        spread(sh2, (row + 4) * 32, values, [16], 32, 4)
    conv_norm(1, sh2, 32, -4, [(0, 13, False), (13, 13, False)], w, nrm)
    mlp(1, sh2, 32, -4, 0, [13, 13], up, down, mask, nrm, keep(x2, 32, 0))


def south_kernel(
    left, own, right, x1_mid, x2_mid, land, mask, w, up, down,
    x1_tail, x2_tail, out, sh1, sh2, sh3, x1, x2, nrm, e1, e2,
):
    clear(sh1, 2 * 32)
    clear(sh2, 4 * 32)
    clear(sh3, 8 * 32)
    for row in range(32):
        spread(sh1, (row + 2) * 32, wide(row, left, own, right), [4, 44], 16, 2)
    cells = spread_mask(land, 0, 30, False)
    e1[...] = jnp.concatenate([cells[:, 4:20], cells[:, 44:60]], axis=1).reshape(30 * 32, 128)
    e2[...] = jnp.concatenate([cells[:26, 8:24], cells[:26, 40:56]], axis=1).reshape(26 * 32, 128)
    conv_norm(0, sh1, 32, -2, [(0, 15, False), (15, 15, False)], w, nrm)
    mlp(0, sh1, 32, -2, 0, [15, 15], up, down, e1, nrm, keep(x1, 32, 0))

    def row1(row):
        at = row * 32
        return jnp.concatenate([x1[at : at + 16], x1_mid[at + 4 : at + 28], x1[at + 16 : at + 32]], axis=0)

    for row in range(30):
        values = row1(row)
        if row >= 22:
            x1_tail[(row - 22) * 56 : (row - 21) * 56] = values
        spread(sh2, (row + 4) * 32, values, [4, 36], 16, 4)
    conv_norm(1, sh2, 32, -4, [(0, 13, False), (13, 13, False)], w, nrm)
    mlp(1, sh2, 32, -4, 0, [13, 13], up, down, e2, nrm, keep(x2, 32, 0))
    for row in range(26):
        at = row * 32
        values = jnp.concatenate([x2[at : at + 16], x2_mid[at + 8 : at + 24], x2[at + 16 : at + 32]], axis=0)
        if row >= 10:
            x2_tail[(row - 10) * 48 : (row - 9) * 48] = values
        spread(sh3, (row + 8) * 32, values, [8], 32, 8)
    conv_norm(2, sh3, 32, -8, [(0, 9, False), (9, 9, False)], w, nrm)

    def store3(row, count, value):
        out[row : row + count] = value.reshape(count, 32, 256)

    mlp(2, sh3, 32, -8, 0, [9, 9], up, down, mask, nrm, store3)


def north_kernel(
    left, own, right, north, north_left, north_right, x1_tail, x2_tail, out_south,
    land, land_north, mask, w, up, down, out, sh1, sh2, sh3, x1, x2, nrm, last, sems, m1, m2,
):
    first = pltpu.make_async_copy(out_south, out.at[0:18], sems.at[0])
    first.start()
    turn = jnp.where(diagonal(True), 1.0, 0.0).astype(BF)
    for row in range(4):
        spread(sh1, row * 56, wide(28 + row, left, own, right), [4], 56, 2)
    for row in range(14):
        source = wide(13 - row, north_right, north, north_left)
        turned = jnp.dot(turn, source, preferred_element_type=F32).astype(BF)
        spread(sh1, (row + 4) * 56, turned, [4], 56, 2)
    near = spread_mask(land, 26, 6, False)
    far = spread_mask(land_north, 0, 14, True)
    for row in range(26, 44):
        cells = near[row - 26] if row < 32 else far[45 - row]
        if row >= 30:
            m1[(row - 30) * 56 : (row - 29) * 56] = cells[4:60]
        if row < 40:
            m2[(row - 26) * 48 : (row - 25) * 48] = cells[8:56]
    conv_norm(0, sh1, 56, 28, [(30, 2, False), (32, 6, True), (38, 6, True)], w, nrm)
    mlp(0, sh1, 56, 28, 30, [8, 6], up, down, m1, nrm, keep(x1, 56, 30), 30)
    for row in range(8):
        spread(sh2, row * 48, x1_tail[row * 56 : (row + 1) * 56], [4], 48, 4)
    for row in range(14):
        spread(sh2, (row + 8) * 48, x1[row * 56 : (row + 1) * 56], [4], 48, 4)
    conv_norm(1, sh2, 48, 22, [(26, 6, False), (32, 8, True)], w, nrm)
    mlp(1, sh2, 48, 22, 26, [7, 7], up, down, m2, nrm, keep(x2, 48, 26), 26)
    for row in range(16):
        spread(sh3, row * 32, x2_tail[row * 48 : (row + 1) * 48], [8], 32, 8)
    for row in range(14):
        spread(sh3, (row + 16) * 32, x2[row * 48 : (row + 1) * 48], [8], 32, 8)
    conv_norm(2, sh3, 32, 10, [(18, 7, False), (25, 7, False)], w, nrm)

    def store3(row, count, value):
        last[row - 18 : row - 18 + count] = value.reshape(count, 32, 256)

    mlp(2, sh3, 32, 10, 18, [7, 7], up, down, mask, nrm, store3)
    second = pltpu.make_async_copy(last, out.at[18:32], sems.at[1])
    second.start()
    first.wait()
    second.wait()


def cost(cells):
    return pl.CostEstimate(
        flops=2 * cells * (9 * 256 * 256 + 2 * 256 * 1024), bytes_accessed=2**20, transcendentals=cells * 1024
    )


VMEM = pl.BlockSpec(memory_space=pltpu.VMEM)
HBM = pl.BlockSpec(memory_space=pltpu.HBM)


def call(kernel, name, outs, in_specs, out_specs, scratch, cells, args, limit=LIMIT):
    return pl.pallas_call(
        kernel,
        name=name,
        out_shape=tuple(jax.ShapeDtypeStruct(*(out if isinstance(out[0], tuple) else (out, BF))) for out in outs),
        in_specs=in_specs,
        out_specs=tuple(out_specs),
        scratch_shapes=scratch,
        compiler_params=pltpu.CompilerParams(vmem_limit_bytes=limit * 2**20),
        cost_estimate=cost(cells),
    )(*args)


def taps(rows, width):
    return pltpu.VMEM((3, rows * width, 256), BF)


def flat(rows, width):
    return pltpu.VMEM((rows * width, 256), BF)


def edges_call(own):
    return call(
        edges_kernel, "edges", [(32, HALO, 256), (32, HALO, 256), (DEEP, 32, 256)], [HBM], [VMEM] * 3,
        [pltpu.SemaphoreType.DMA((3,))], EDGE_CELLS, (own,),
    )


def first_call(*args):
    return call(
        first_kernel, "first", [(30 * 32, 256), (32 * 32, 128), ((32, 64), F32), ((DEEP, 64), F32)],
        [VMEM] * len(args), [VMEM] * 4, [taps(34, 32), flat(30, 32)], 960, args,
    )


def second_call(*args):
    (x2,) = call(
        second_kernel, "second", [(26 * 32, 256)], [VMEM] * len(args), [VMEM], [taps(34, 32), flat(26, 32)], 832, args
    )
    return x2


def south_call(*args):
    return call(
        south_kernel, "south", [(8 * 56, 256), (16 * 48, 256), (18, 32, 256)], [VMEM] * len(args), [VMEM] * 3,
        [taps(34, 32), taps(34, 32), taps(34, 32), flat(30, 32), flat(26, 32), flat(30, 32),
         pltpu.VMEM((30 * 32, 128), BF), pltpu.VMEM((26 * 32, 128), BF)],
        2368, args,
    )


def north_call(*args):
    (out,) = call(
        north_kernel, "north", [(32, 32, 256)], [VMEM] * len(args), [HBM],
        [
            taps(18, 56), taps(22, 48), taps(30, 32), flat(14, 56), flat(14, 48), flat(14, 56),
            pltpu.VMEM((14, 32, 256), BF), pltpu.SemaphoreType.DMA((2,)),
            pltpu.VMEM((14 * 56, 128), BF), pltpu.VMEM((14 * 48, 128), BF),
        ],
        1904, args,
    )
    return out


def around(value, step):
    count = lax.axis_size("lon")
    return lax.ppermute(value, "lon", [(i, (i + step) % count) for i in range(count)])


def per_device(own, land_sea, w, up, down):
    count = lax.axis_size("lon")
    cols = own.shape[1]
    head, tail, top = edges_call(own)
    left = around(tail, 1)
    right = around(head, -1)
    weights = (w, up, down)
    x1_mid, mask, land, land_north = first_call(own, land_sea, *weights)
    top, x1_mid = lax.optimization_barrier((top, x1_mid))
    north = lax.ppermute(top, "lon", [(i, count - 1 - i) for i in range(count)])
    x2_mid = second_call(x1_mid, mask, *weights)
    x1_tail, x2_tail, out_south = south_call(left, own, right, x1_mid, x2_mid, land, mask, *weights)
    north, x1_tail = lax.optimization_barrier((north, x1_tail))
    north_left = around(north[:, :HALO], 1)
    north_right = around(north[:, cols - HALO :], -1)
    return north_call(
        left, own, right, north, north_left, north_right, x1_tail, x2_tail, out_south, land, land_north, mask, *weights
    )


def solution(mesh):
    in_specs = (P("parts", "lon", None), P(), P(), P(), P())
    out_specs = P("parts", "lon", None)
    return jax.shard_map(
        per_device, mesh=mesh, in_specs=in_specs, out_specs=out_specs, check_vma=False
    )
```

```python
import functools

import jax
import jax.numpy as jnp
import numpy as np
from jax import lax
from jax.experimental import pallas as pl
from jax.experimental.pallas import tpu as pltpu
from jax.sharding import PartitionSpec as P

BF = jnp.bfloat16
F32 = jnp.float32
HALO = 16
DEEP = 14
LIMIT = 20
EDGE_CELLS = 2048
RSQRT2 = np.float32(0.7071067811865476)


def conv_norm(layer, shifted, width, base, chunks, w_ref, nrm):
    dil = 2 ** (layer + 1)
    weight = w_ref[layer].reshape(-1, w_ref.shape[-1])
    at = 0
    for first, count, turned in chunks:
        taps = [(a, b) for a in range(3) for b in range(3)]
        if turned:
            taps = taps[::-1]
        size = count * width
        lhs = jnp.concatenate(
            [
                shifted[b, (first - base + (a - 1) * dil) * width : (first - base + (a - 1) * dil) * width + size]
                for a, b in taps
            ],
            axis=1,
        )
        conv = jnp.dot(lhs, weight, preferred_element_type=F32)
        mean = jnp.mean(conv, axis=-1, keepdims=True)
        centred = conv - mean
        var = jnp.mean(centred * centred, axis=-1, keepdims=True)
        nrm[at : at + size] = (centred * lax.rsqrt(var + 1e-05)).astype(BF)
        at += size


def mlp(layer, shifted, width, base, first, counts, up_ref, down_ref, mask_ref, nrm, store, mask_base=0):
    at = 0
    row = first
    for count in counts:
        size = count * width
        pre = jnp.dot(nrm[at : at + size], up_ref[layer], preferred_element_type=F32)
        hidden = (0.5 * pre * (1.0 + lax.erf(pre * RSQRT2))).astype(BF)
        branch = jnp.dot(hidden, down_ref[layer], preferred_element_type=F32)
        centre = shifted[1, (row - base) * width : (row - base) * width + size].astype(F32)
        mask = mask_ref[(row - mask_base) * width : (row - mask_base) * width + size].astype(F32)
        mask = jnp.concatenate([mask, mask], axis=1)
        store(row, count, (mask * (centre + branch)).astype(BF))
        at += size
        row += count


def spread(shifted, at, values, starts, size, dil):
    for b in range(3):
        for k, start in enumerate(starts):
            lo = start + (b - 1) * dil
            shifted[b, at + k * size : at + (k + 1) * size] = values[lo : lo + size]


def clear(shifted, size):
    for b in range(3):
        shifted[b, :size] = jnp.zeros((size, shifted.shape[-1]), BF)


def keep(ref, width, base):
    def store(row, count, value):
        ref[(row - base) * width : (row - base + count) * width] = value

    return store


def diagonal(turned, size=64):
    rows = lax.broadcasted_iota(jnp.int32, (size, size), 0)
    cols = lax.broadcasted_iota(jnp.int32, (size, size), 1)
    return rows + cols == size - 1 if turned else rows == cols


def spread_mask(land, first, count, turned):
    lines = jnp.where(diagonal(turned)[None], land[first : first + count][:, None, :], 0.0).astype(BF)
    cells = jnp.dot(lines.reshape(count * 64, 64), jnp.ones((64, 128), BF), preferred_element_type=F32)
    return cells.astype(BF).reshape(count, 64, 128)


def window(whole, first):
    total = whole.shape[1]
    source = lax.broadcasted_iota(jnp.int32, (total, 64), 0)
    target = lax.broadcasted_iota(jnp.int32, (total, 64), 1) + first
    target = jnp.where(target < 0, target + total, target)
    target = jnp.where(target >= total, target - total, target)
    pick = jnp.where(source == target, 1.0, 0.0).astype(BF)
    return jnp.dot(whole, pick, preferred_element_type=F32)


def edges_kernel(own, left, right, top, sems):
    copies = [
        pltpu.make_async_copy(own.at[:, 0:HALO], left, sems.at[0]),
        pltpu.make_async_copy(own.at[:, 32 - HALO : 32], right, sems.at[1]),
        pltpu.make_async_copy(own.at[32 - DEEP : 32], top, sems.at[2]),
    ]
    for copy in copies:
        copy.start()
    for copy in copies:
        copy.wait()


def wide(row, left, own, right):
    return jnp.concatenate([left[row], own[row], right[row]], axis=0)


def first_kernel(own, land_sea, w, up, down, x1, mask, land, land_north, sh1, nrm):
    me = lax.axis_index("lon")
    whole = land_sea[...].astype(F32).astype(BF)
    land[...] = window(whole, me * 32 - HALO)
    land_north[...] = window(whole, (lax.axis_size("lon") - 1 - me) * 32 - HALO)[32 - DEEP :]
    mask[...] = spread_mask(land, 0, 32, False)[:, 16:48].reshape(32 * 32, 128)
    clear(sh1, 2 * 32)
    edge = jnp.zeros((HALO, own.shape[-1]), BF)
    for row in range(32):
        spread(sh1, (row + 2) * 32, jnp.concatenate([edge, own[row], edge], axis=0), [16], 32, 2)
    conv_norm(0, sh1, 32, -2, [(0, 15, False), (15, 15, False)], w, nrm)
    mlp(0, sh1, 32, -2, 0, [15, 15], up, down, mask, nrm, keep(x1, 32, 0))


def second_kernel(x1, mask, w, up, down, x2, sh2, nrm):
    clear(sh2, 4 * 32)
    edge = jnp.zeros((HALO, x1.shape[-1]), BF)
    for row in range(30):
        values = jnp.concatenate([edge, x1[row * 32 : (row + 1) * 32], edge], axis=0)
        spread(sh2, (row + 4) * 32, values, [16], 32, 4)
    conv_norm(1, sh2, 32, -4, [(0, 13, False), (13, 13, False)], w, nrm)
    mlp(1, sh2, 32, -4, 0, [13, 13], up, down, mask, nrm, keep(x2, 32, 0))


def south_kernel(
    left, own, right, x1_mid, x2_mid, land, mask, w, up, down,
    x1_tail, x2_tail, out, sh1, sh2, sh3, x1, x2, nrm, e1, e2,
):
    clear(sh1, 2 * 32)
    clear(sh2, 4 * 32)
    clear(sh3, 8 * 32)
    for row in range(32):
        spread(sh1, (row + 2) * 32, wide(row, left, own, right), [4, 44], 16, 2)
    cells = spread_mask(land, 0, 30, False)
    e1[...] = jnp.concatenate([cells[:, 4:20], cells[:, 44:60]], axis=1).reshape(30 * 32, 128)
    e2[...] = jnp.concatenate([cells[:26, 8:24], cells[:26, 40:56]], axis=1).reshape(26 * 32, 128)
    conv_norm(0, sh1, 32, -2, [(0, 15, False), (15, 15, False)], w, nrm)
    mlp(0, sh1, 32, -2, 0, [15, 15], up, down, e1, nrm, keep(x1, 32, 0))

    def row1(row):
        at = row * 32
        return jnp.concatenate([x1[at : at + 16], x1_mid[at + 4 : at + 28], x1[at + 16 : at + 32]], axis=0)

    for row in range(30):
        values = row1(row)
        if row >= 22:
            x1_tail[(row - 22) * 56 : (row - 21) * 56] = values
        spread(sh2, (row + 4) * 32, values, [4, 36], 16, 4)
    conv_norm(1, sh2, 32, -4, [(0, 13, False), (13, 13, False)], w, nrm)
    mlp(1, sh2, 32, -4, 0, [13, 13], up, down, e2, nrm, keep(x2, 32, 0))
    for row in range(26):
        at = row * 32
        values = jnp.concatenate([x2[at : at + 16], x2_mid[at + 8 : at + 24], x2[at + 16 : at + 32]], axis=0)
        if row >= 10:
            x2_tail[(row - 10) * 48 : (row - 9) * 48] = values
        spread(sh3, (row + 8) * 32, values, [8], 32, 8)
    conv_norm(2, sh3, 32, -8, [(0, 9, False), (9, 9, False)], w, nrm)

    def store3(row, count, value):
        out[row : row + count] = value.reshape(count, 32, 256)

    mlp(2, sh3, 32, -8, 0, [9, 9], up, down, mask, nrm, store3)


def strips(cells, left, right):
    rows = cells.shape[0]
    return jnp.concatenate([cells[:, left : left + 16], cells[:, right : right + 16]], axis=1).reshape(rows * 32, 128)


def fold_kernel(own, north, x1_tail, land, land_north, w, up, down, x1, x2, e1, e2, sh1, sh2, nrm, m1, m2):
    near = spread_mask(land, 26, 6, False)
    far = spread_mask(land_north, 0, DEEP, True)
    cells = jnp.concatenate([near] + [far[45 - row : 46 - row] for row in range(32, 44)], axis=0)
    m1[...] = cells[4:, 16:48].reshape(14 * 32, 128)
    m2[...] = cells[:14, 16:48].reshape(14 * 32, 128)
    e1[...] = strips(cells[4:], 4, 44)
    e2[...] = strips(cells[:14], 8, 40)
    turn = jnp.where(diagonal(True, 32), 1.0, 0.0).astype(BF)
    edge = jnp.zeros((HALO, own.shape[-1]), BF)
    for row in range(18):
        if row < 4:
            line = own[28 + row]
        else:
            line = jnp.dot(turn, north[17 - row], preferred_element_type=F32).astype(BF)
        spread(sh1, row * 32, jnp.concatenate([edge, line, edge], axis=0), [16], 32, 2)
    conv_norm(0, sh1, 32, 28, [(30, 2, False), (32, 12, True)], w, nrm)
    mlp(0, sh1, 32, 28, 30, [7, 7], up, down, m1, nrm, keep(x1, 32, 30), 30)
    for row in range(8):
        spread(sh2, row * 32, x1_tail[row * 56 : (row + 1) * 56], [12], 32, 4)
    for row in range(14):
        values = jnp.concatenate([edge, x1[row * 32 : (row + 1) * 32], edge], axis=0)
        spread(sh2, (row + 8) * 32, values, [16], 32, 4)
    conv_norm(1, sh2, 32, 22, [(26, 6, False), (32, 8, True)], w, nrm)
    mlp(1, sh2, 32, 22, 26, [7, 7], up, down, m2, nrm, keep(x2, 32, 26), 26)


def north_kernel(
    left, own, right, north, north_left, north_right, x1_tail, x2_tail, out_south, x1_mid, x2_mid,
    e1, e2, mask, w, up, down, out, sh1, sh2, sh3, x1, x2, nrm, last, sems,
):
    first = pltpu.make_async_copy(out_south, out.at[0:18], sems.at[0])
    first.start()
    half = lax.axis_size("lon") // 2
    place = lax.rem(lax.axis_index("lon"), half)
    turn = jnp.where(diagonal(True), 1.0, 0.0).astype(BF)
    for row in range(4):
        spread(sh1, row * 32, wide(28 + row, left, own, right), [4, 44], 16, 2)
    for row in range(14):
        at = 13 - row
        after = jnp.where(place == 0, own[18 + at, 0:HALO], north_left[at])
        before = jnp.where(place == half - 1, own[18 + at, 32 - HALO : 32], north_right[at])
        source = jnp.concatenate([before, north[at], after], axis=0)
        turned = jnp.dot(turn, source, preferred_element_type=F32).astype(BF)
        spread(sh1, (row + 4) * 32, turned, [4, 44], 16, 2)
    conv_norm(0, sh1, 32, 28, [(30, 2, False), (32, 12, True)], w, nrm)
    mlp(0, sh1, 32, 28, 30, [7, 7], up, down, e1, nrm, keep(x1, 32, 30), 30)
    for row in range(8):
        spread(sh2, row * 32, x1_tail[row * 56 : (row + 1) * 56], [4, 36], 16, 4)
    for row in range(14):
        at = row * 32
        values = jnp.concatenate([x1[at : at + 16], x1_mid[at + 4 : at + 28], x1[at + 16 : at + 32]], axis=0)
        spread(sh2, (row + 8) * 32, values, [4, 36], 16, 4)
    conv_norm(1, sh2, 32, 22, [(26, 6, False), (32, 8, True)], w, nrm)
    mlp(1, sh2, 32, 22, 26, [7, 7], up, down, e2, nrm, keep(x2, 32, 26), 26)
    for row in range(16):
        spread(sh3, row * 32, x2_tail[row * 48 : (row + 1) * 48], [8], 32, 8)
    for row in range(14):
        at = row * 32
        values = jnp.concatenate([x2[at : at + 16], x2_mid[at + 8 : at + 24], x2[at + 16 : at + 32]], axis=0)
        spread(sh3, (row + 16) * 32, values, [8], 32, 8)
    conv_norm(2, sh3, 32, 10, [(18, 14, False)], w, nrm)

    def store3(row, count, value):
        last[row - 18 : row - 18 + count] = value.reshape(count, 32, 256)

    mlp(2, sh3, 32, 10, 18, [7, 7], up, down, mask, nrm, store3)
    second = pltpu.make_async_copy(last, out.at[18:32], sems.at[1])
    second.start()
    first.wait()
    second.wait()


def cost(cells):
    return pl.CostEstimate(
        flops=2 * cells * (9 * 256 * 256 + 2 * 256 * 1024), bytes_accessed=2**20, transcendentals=cells * 1024
    )


VMEM = pl.BlockSpec(memory_space=pltpu.VMEM)
HBM = pl.BlockSpec(memory_space=pltpu.HBM)


def call(kernel, name, outs, in_specs, out_specs, scratch, cells, args, limit=LIMIT):
    return pl.pallas_call(
        kernel,
        name=name,
        out_shape=tuple(jax.ShapeDtypeStruct(*(out if isinstance(out[0], tuple) else (out, BF))) for out in outs),
        in_specs=in_specs,
        out_specs=tuple(out_specs),
        scratch_shapes=scratch,
        compiler_params=pltpu.CompilerParams(vmem_limit_bytes=limit * 2**20),
        cost_estimate=cost(cells),
    )(*args)


def taps(rows, width):
    return pltpu.VMEM((3, rows * width, 256), BF)


def flat(rows, width):
    return pltpu.VMEM((rows * width, 256), BF)


def edges_call(own):
    return call(
        edges_kernel, "edges", [(32, HALO, 256), (32, HALO, 256), (DEEP, 32, 256)], [HBM], [VMEM] * 3,
        [pltpu.SemaphoreType.DMA((3,))], EDGE_CELLS, (own,),
    )


def first_call(*args):
    return call(
        first_kernel, "first", [(30 * 32, 256), (32 * 32, 128), ((32, 64), F32), ((DEEP, 64), F32)],
        [VMEM] * len(args), [VMEM] * 4, [taps(34, 32), flat(30, 32)], 960, args,
    )


def second_call(*args):
    (x2,) = call(
        second_kernel, "second", [(26 * 32, 256)], [VMEM] * len(args), [VMEM], [taps(34, 32), flat(26, 32)], 832, args
    )
    return x2


def south_call(*args):
    return call(
        south_kernel, "south", [(8 * 56, 256), (16 * 48, 256), (18, 32, 256)], [VMEM] * len(args), [VMEM] * 3,
        [taps(34, 32), taps(34, 32), taps(34, 32), flat(30, 32), flat(26, 32), flat(30, 32),
         pltpu.VMEM((30 * 32, 128), BF), pltpu.VMEM((26 * 32, 128), BF)],
        2368, args,
    )


def fold_call(*args):
    return call(
        fold_kernel, "fold", [(14 * 32, 256), (14 * 32, 256), (14 * 32, 128), (14 * 32, 128)],
        [VMEM] * len(args), [VMEM] * 4,
        [taps(18, 32), taps(22, 32), flat(14, 32), pltpu.VMEM((14 * 32, 128), BF), pltpu.VMEM((14 * 32, 128), BF)],
        896, args,
    )


def north_call(*args):
    (out,) = call(
        north_kernel, "north", [(32, 32, 256)], [VMEM] * len(args), [HBM],
        [
            taps(18, 32), taps(22, 32), taps(30, 32), flat(14, 32), flat(14, 32), flat(14, 32),
            pltpu.VMEM((14, 32, 256), BF), pltpu.SemaphoreType.DMA((2,)),
        ],
        1344, args,
    )
    return out


def around(value, step, ring=1):
    count = lax.axis_size("lon") // ring
    pairs = [(i, i // count * count + (i + step) % count) for i in range(ring * count)]
    return lax.ppermute(value, "lon", pairs)


def per_device(own, land_sea, w, up, down):
    count = lax.axis_size("lon")
    cols = own.shape[1]
    head, tail, top = edges_call(own)
    left = around(tail, 1)
    right = around(head, -1)
    weights = (w, up, down)
    x1_mid, mask, land, land_north = first_call(own, land_sea, *weights)
    top, x1_mid = lax.optimization_barrier((top, x1_mid))
    north = lax.ppermute(top, "lon", [(i, count - 1 - i) for i in range(count)])
    x2_mid = second_call(x1_mid, mask, *weights)
    x1_tail, x2_tail, out_south = south_call(left, own, right, x1_mid, x2_mid, land, mask, *weights)
    north, x1_tail = lax.optimization_barrier((north, x1_tail))
    north_left = around(north[:, :HALO], 1, 2)
    north_right = around(north[:, cols - HALO :], -1, 2)
    y1_mid, y2_mid, e1, e2 = fold_call(own, north, x1_tail, land, land_north, *weights)
    return north_call(
        left, own, right, north, north_left, north_right, x1_tail, x2_tail, out_south, y1_mid, y2_mid, e1, e2, mask, *weights
    )


def solution(mesh):
    in_specs = (P("parts", "lon", None), P(), P(), P(), P())
    out_specs = P("parts", "lon", None)
    return jax.shard_map(
        per_device, mesh=mesh, in_specs=in_specs, out_specs=out_specs, check_vma=False
    )
```

```python
import functools

import jax
import jax.numpy as jnp
import numpy as np
from jax import lax
from jax.experimental import pallas as pl
from jax.experimental.pallas import tpu as pltpu
from jax.sharding import PartitionSpec as P

BF = jnp.bfloat16
F32 = jnp.float32
HALO = 16
DEEP = 14
LIMIT = 20
EDGE_CELLS = 2048
RSQRT2 = np.float32(0.7071067811865476)


def conv_norm(layer, shifted, width, base, chunks, w_ref, nrm):
    dil = 2 ** (layer + 1)
    weight = w_ref[layer].reshape(-1, w_ref.shape[-1])
    at = 0
    for first, count, turned in chunks:
        taps = [(a, b) for a in range(3) for b in range(3)]
        if turned:
            taps = taps[::-1]
        size = count * width
        lhs = jnp.concatenate(
            [
                shifted[b, (first - base + (a - 1) * dil) * width : (first - base + (a - 1) * dil) * width + size]
                for a, b in taps
            ],
            axis=1,
        )
        conv = jnp.dot(lhs, weight, preferred_element_type=F32)
        mean = jnp.mean(conv, axis=-1, keepdims=True)
        centred = conv - mean
        var = jnp.mean(centred * centred, axis=-1, keepdims=True)
        nrm[at : at + size] = (centred * lax.rsqrt(var + 1e-05)).astype(BF)
        at += size


def mlp(layer, shifted, width, base, first, counts, up_ref, down_ref, mask_ref, nrm, store, mask_base=0):
    at = 0
    row = first
    for count in counts:
        size = count * width
        pre = jnp.dot(nrm[at : at + size], up_ref[layer], preferred_element_type=F32)
        hidden = (0.5 * pre * (1.0 + lax.erf(pre * RSQRT2))).astype(BF)
        branch = jnp.dot(hidden, down_ref[layer], preferred_element_type=F32)
        centre = shifted[1, (row - base) * width : (row - base) * width + size].astype(F32)
        mask = mask_ref[(row - mask_base) * width : (row - mask_base) * width + size].astype(F32)
        mask = jnp.concatenate([mask, mask], axis=1)
        store(row, count, (mask * (centre + branch)).astype(BF))
        at += size
        row += count


def spread(shifted, at, values, starts, size, dil):
    for b in range(3):
        for k, start in enumerate(starts):
            lo = start + (b - 1) * dil
            shifted[b, at + k * size : at + (k + 1) * size] = values[lo : lo + size]


def clear(shifted, size):
    for b in range(3):
        shifted[b, :size] = jnp.zeros((size, shifted.shape[-1]), BF)


def keep(ref, width, base):
    def store(row, count, value):
        ref[(row - base) * width : (row - base + count) * width] = value

    return store


def diagonal(turned, size=64):
    rows = lax.broadcasted_iota(jnp.int32, (size, size), 0)
    cols = lax.broadcasted_iota(jnp.int32, (size, size), 1)
    return rows + cols == size - 1 if turned else rows == cols


def spread_mask(land, first, count, turned):
    lines = jnp.where(diagonal(turned)[None], land[first : first + count][:, None, :], 0.0).astype(BF)
    cells = jnp.dot(lines.reshape(count * 64, 64), jnp.ones((64, 128), BF), preferred_element_type=F32)
    return cells.astype(BF).reshape(count, 64, 128)


def window(whole, first):
    total = whole.shape[1]
    source = lax.broadcasted_iota(jnp.int32, (total, 64), 0)
    target = lax.broadcasted_iota(jnp.int32, (total, 64), 1) + first
    target = jnp.where(target < 0, target + total, target)
    target = jnp.where(target >= total, target - total, target)
    pick = jnp.where(source == target, 1.0, 0.0).astype(BF)
    return jnp.dot(whole, pick, preferred_element_type=F32)


def edges_kernel(own, left, right, top, sems):
    copies = [
        pltpu.make_async_copy(own.at[:, 0:HALO], left, sems.at[0]),
        pltpu.make_async_copy(own.at[:, 32 - HALO : 32], right, sems.at[1]),
        pltpu.make_async_copy(own.at[32 - DEEP : 32], top, sems.at[2]),
    ]
    for copy in copies:
        copy.start()
    for copy in copies:
        copy.wait()


def wide(row, left, own, right):
    return jnp.concatenate([left[row], own[row], right[row]], axis=0)


def first_kernel(own, land_sea, w, up, down, x1, mask, land, land_north, sh1, nrm, m1):
    me = lax.axis_index("lon")
    whole = land_sea[...].astype(F32).astype(BF)
    land[...] = window(whole, me * 32 - HALO)
    land_north[...] = window(whole, (lax.axis_size("lon") - 1 - me) * 32 - HALO)[32 - DEEP :]
    cells = spread_mask(land, 0, 32, False)
    mask[...] = cells[:, 16:48].reshape(32 * 32, 128)
    m1[...] = cells[:30, 20:44].reshape(30 * 24, 128)
    clear(sh1, 2 * 24)
    for row in range(32):
        spread(sh1, (row + 2) * 24, own[row], [4], 24, 2)
    conv_norm(0, sh1, 24, -2, [(0, 8, False), (8, 8, False), (16, 8, False), (24, 6, False)], w, nrm)
    mlp(0, sh1, 24, -2, 0, [16, 14], up, down, m1, nrm, keep(x1, 24, 0))


def second_kernel(x1, mask, w, up, down, x2, sh2, nrm, m2):
    for row in range(26):
        m2[row * 16 : (row + 1) * 16] = mask[row * 32 + 8 : row * 32 + 24]
    clear(sh2, 4 * 16)
    for row in range(30):
        spread(sh2, (row + 4) * 16, x1[row * 24 : (row + 1) * 24], [4], 16, 4)
    conv_norm(1, sh2, 16, -4, [(0, 13, False), (13, 13, False)], w, nrm)
    mlp(1, sh2, 16, -4, 0, [26], up, down, m2, nrm, keep(x2, 16, 0))


def south_kernel(
    left, own, right, x1_mid, x2_mid, land, mask, w, up, down,
    x1_tail, x2_tail, out, sh1, sh2, sh3, x1, x2, nrm, e1, e2,
):
    clear(sh1, 2 * 32)
    clear(sh2, 4 * 32)
    clear(sh3, 8 * 32)
    for row in range(32):
        spread(sh1, (row + 2) * 32, wide(row, left, own, right), [4, 44], 16, 2)
    cells = spread_mask(land, 0, 30, False)
    e1[...] = jnp.concatenate([cells[:, 4:20], cells[:, 44:60]], axis=1).reshape(30 * 32, 128)
    e2[...] = jnp.concatenate([cells[:26, 8:24], cells[:26, 40:56]], axis=1).reshape(26 * 32, 128)
    conv_norm(0, sh1, 32, -2, [(0, 8, False), (8, 8, False), (16, 7, False), (23, 7, False)], w, nrm)
    mlp(0, sh1, 32, -2, 0, [15, 15], up, down, e1, nrm, keep(x1, 32, 0))

    def row1(row):
        at = row * 32
        return jnp.concatenate([x1[at : at + 16], x1_mid[row * 24 : (row + 1) * 24], x1[at + 16 : at + 32]], axis=0)

    for row in range(30):
        values = row1(row)
        if row >= 22:
            x1_tail[(row - 22) * 56 : (row - 21) * 56] = values
        spread(sh2, (row + 4) * 32, values, [4, 36], 16, 4)
    conv_norm(1, sh2, 32, -4, [(0, 7, False), (7, 7, False), (14, 6, False), (20, 6, False)], w, nrm)
    mlp(1, sh2, 32, -4, 0, [13, 13], up, down, e2, nrm, keep(x2, 32, 0))
    for row in range(26):
        at = row * 32
        values = jnp.concatenate([x2[at : at + 16], x2_mid[row * 16 : (row + 1) * 16], x2[at + 16 : at + 32]], axis=0)
        if row >= 10:
            x2_tail[(row - 10) * 48 : (row - 9) * 48] = values
        spread(sh3, (row + 8) * 32, values, [8], 32, 8)
    conv_norm(2, sh3, 32, -8, [(0, 6, False), (6, 6, False), (12, 6, False)], w, nrm)

    def store3(row, count, value):
        out[row : row + count] = value.reshape(count, 32, 256)

    mlp(2, sh3, 32, -8, 0, [9, 9], up, down, mask, nrm, store3)


def strips(cells, left, right):
    rows = cells.shape[0]
    return jnp.concatenate([cells[:, left : left + 16], cells[:, right : right + 16]], axis=1).reshape(rows * 32, 128)


def fold_kernel(own, north, x1_tail, land, land_north, w, up, down, x1, x2, e1, e2, sh1, sh2, nrm, m1, m2):
    near = spread_mask(land, 26, 6, False)
    far = spread_mask(land_north, 0, DEEP, True)
    cells = jnp.concatenate([near] + [far[45 - row : 46 - row] for row in range(32, 44)], axis=0)
    m1[...] = cells[4:, 20:44].reshape(14 * 24, 128)
    m2[...] = cells[:14, 24:40].reshape(14 * 16, 128)
    e1[...] = strips(cells[4:], 4, 44)
    e2[...] = strips(cells[:14], 8, 40)
    turn = jnp.where(diagonal(True, 32), 1.0, 0.0).astype(BF)
    for row in range(18):
        if row < 4:
            line = own[28 + row]
        else:
            line = jnp.dot(turn, north[17 - row], preferred_element_type=F32).astype(BF)
        spread(sh1, row * 24, line, [4], 24, 2)
    conv_norm(0, sh1, 24, 28, [(30, 2, False), (32, 6, True), (38, 6, True)], w, nrm)
    mlp(0, sh1, 24, 28, 30, [8, 6], up, down, m1, nrm, keep(x1, 24, 30), 30)
    for row in range(8):
        spread(sh2, row * 16, x1_tail[row * 56 : (row + 1) * 56], [20], 16, 4)
    for row in range(14):
        spread(sh2, (row + 8) * 16, x1[row * 24 : (row + 1) * 24], [4], 16, 4)
    conv_norm(1, sh2, 16, 22, [(26, 6, False), (32, 8, True)], w, nrm)
    mlp(1, sh2, 16, 22, 26, [7, 7], up, down, m2, nrm, keep(x2, 16, 26), 26)


def north_kernel(
    left, own, right, north, north_left, north_right, x1_tail, x2_tail, out_south, x1_mid, x2_mid,
    e1, e2, mask, w, up, down, out, sh1, sh2, sh3, x1, x2, nrm, last, sems,
):
    first = pltpu.make_async_copy(out_south, out.at[0:18], sems.at[0])
    first.start()
    half = lax.axis_size("lon") // 2
    place = lax.rem(lax.axis_index("lon"), half)
    turn = jnp.where(diagonal(True), 1.0, 0.0).astype(BF)
    for row in range(4):
        spread(sh1, row * 32, wide(28 + row, left, own, right), [4, 44], 16, 2)
    for row in range(14):
        at = 13 - row
        after = jnp.where(place == 0, own[18 + at, 0:HALO], north_left[at])
        before = jnp.where(place == half - 1, own[18 + at, 32 - HALO : 32], north_right[at])
        source = jnp.concatenate([before, north[at], after], axis=0)
        turned = jnp.dot(turn, source, preferred_element_type=F32).astype(BF)
        spread(sh1, (row + 4) * 32, turned, [4, 44], 16, 2)
    conv_norm(0, sh1, 32, 28, [(30, 2, False), (32, 6, True), (38, 6, True)], w, nrm)
    mlp(0, sh1, 32, 28, 30, [7, 7], up, down, e1, nrm, keep(x1, 32, 30), 30)
    for row in range(8):
        spread(sh2, row * 32, x1_tail[row * 56 : (row + 1) * 56], [4, 36], 16, 4)
    for row in range(14):
        at = row * 32
        values = jnp.concatenate([x1[at : at + 16], x1_mid[row * 24 : (row + 1) * 24], x1[at + 16 : at + 32]], axis=0)
        spread(sh2, (row + 8) * 32, values, [4, 36], 16, 4)
    conv_norm(1, sh2, 32, 22, [(26, 6, False), (32, 8, True)], w, nrm)
    mlp(1, sh2, 32, 22, 26, [7, 7], up, down, e2, nrm, keep(x2, 32, 26), 26)
    for row in range(16):
        spread(sh3, row * 32, x2_tail[row * 48 : (row + 1) * 48], [8], 32, 8)
    for row in range(14):
        at = row * 32
        values = jnp.concatenate([x2[at : at + 16], x2_mid[row * 16 : (row + 1) * 16], x2[at + 16 : at + 32]], axis=0)
        spread(sh3, (row + 16) * 32, values, [8], 32, 8)
    conv_norm(2, sh3, 32, 10, [(18, 7, False), (25, 7, False)], w, nrm)

    copies = [first]

    def store3(row, count, value):
        last[row - 18 : row - 18 + count] = value.reshape(count, 32, 256)
        here = pltpu.make_async_copy(
            last.at[row - 18 : row - 18 + count], out.at[row : row + count], sems.at[len(copies)]
        )
        here.start()
        copies.append(here)

    mlp(2, sh3, 32, 10, 18, [7, 7], up, down, mask, nrm, store3)
    for copy in copies:
        copy.wait()


def cost(cells):
    return pl.CostEstimate(
        flops=2 * cells * (9 * 256 * 256 + 2 * 256 * 1024), bytes_accessed=2**20, transcendentals=cells * 1024
    )


VMEM = pl.BlockSpec(memory_space=pltpu.VMEM)
HBM = pl.BlockSpec(memory_space=pltpu.HBM)


def call(kernel, name, outs, in_specs, out_specs, scratch, cells, args, limit=LIMIT):
    return pl.pallas_call(
        kernel,
        name=name,
        out_shape=tuple(jax.ShapeDtypeStruct(*(out if isinstance(out[0], tuple) else (out, BF))) for out in outs),
        in_specs=in_specs,
        out_specs=tuple(out_specs),
        scratch_shapes=scratch,
        compiler_params=pltpu.CompilerParams(vmem_limit_bytes=limit * 2**20),
        cost_estimate=cost(cells),
    )(*args)


def taps(rows, width):
    return pltpu.VMEM((3, rows * width, 256), BF)


def flat(rows, width):
    return pltpu.VMEM((rows * width, 256), BF)


def edges_call(own):
    return call(
        edges_kernel, "edges", [(32, HALO, 256), (32, HALO, 256), (DEEP, 32, 256)], [HBM], [VMEM] * 3,
        [pltpu.SemaphoreType.DMA((3,))], EDGE_CELLS, (own,),
    )


def first_call(*args):
    return call(
        first_kernel, "first", [(30 * 24, 256), (32 * 32, 128), ((32, 64), F32), ((DEEP, 64), F32)],
        [VMEM] * len(args), [VMEM] * 4,
        [taps(34, 24), flat(30, 24), pltpu.VMEM((30 * 24, 128), BF)], 720, args,
    )


def second_call(*args):
    (x2,) = call(
        second_kernel, "second", [(26 * 16, 256)], [VMEM] * len(args), [VMEM],
        [taps(34, 16), flat(26, 16), pltpu.VMEM((26 * 16, 128), BF)], 416, args,
    )
    return x2


def south_call(*args):
    return call(
        south_kernel, "south", [(8 * 56, 256), (16 * 48, 256), (18, 32, 256)], [VMEM] * len(args), [VMEM] * 3,
        [taps(34, 32), taps(34, 32), taps(34, 32), flat(30, 32), flat(26, 32), flat(30, 32),
         pltpu.VMEM((30 * 32, 128), BF), pltpu.VMEM((26 * 32, 128), BF)],
        2368, args,
    )


def fold_call(*args):
    return call(
        fold_kernel, "fold", [(14 * 24, 256), (14 * 16, 256), (14 * 32, 128), (14 * 32, 128)],
        [VMEM] * len(args), [VMEM] * 4,
        [taps(18, 24), taps(22, 16), flat(14, 24), pltpu.VMEM((14 * 24, 128), BF), pltpu.VMEM((14 * 16, 128), BF)],
        560, args,
    )


def north_call(*args):
    (out,) = call(
        north_kernel, "north", [(32, 32, 256)], [VMEM] * len(args), [HBM],
        [
            taps(18, 32), taps(22, 32), taps(30, 32), flat(14, 32), flat(14, 32), flat(14, 32),
            pltpu.VMEM((14, 32, 256), BF), pltpu.SemaphoreType.DMA((3,)),
        ],
        1344, args,
    )
    return out


def around(value, step, ring=1):
    count = lax.axis_size("lon") // ring
    pairs = [(i, i // count * count + (i + step) % count) for i in range(ring * count)]
    return lax.ppermute(value, "lon", pairs)


def per_device(own, land_sea, w, up, down):
    count = lax.axis_size("lon")
    cols = own.shape[1]
    head, tail, top = edges_call(own)
    left = around(tail, 1)
    right = around(head, -1)
    weights = (w, up, down)
    x1_mid, mask, land, land_north = first_call(own, land_sea, *weights)
    top, x1_mid = lax.optimization_barrier((top, x1_mid))
    north = lax.ppermute(top, "lon", [(i, count - 1 - i) for i in range(count)])
    x2_mid = second_call(x1_mid, mask, *weights)
    x1_tail, x2_tail, out_south = south_call(left, own, right, x1_mid, x2_mid, land, mask, *weights)
    north, x1_tail = lax.optimization_barrier((north, x1_tail))
    north_left = around(north[:, :HALO], 1, 2)
    north_right = around(north[:, cols - HALO :], -1, 2)
    y1_mid, y2_mid, e1, e2 = fold_call(own, north, x1_tail, land, land_north, *weights)
    return north_call(
        left, own, right, north, north_left, north_right, x1_tail, x2_tail, out_south, y1_mid, y2_mid, e1, e2, mask, *weights
    )


def solution(mesh):
    in_specs = (P("parts", "lon", None), P(), P(), P(), P())
    out_specs = P("parts", "lon", None)
    return jax.shard_map(
        per_device, mesh=mesh, in_specs=in_specs, out_specs=out_specs, check_vma=False
    )
```

```python
import functools

import jax
import jax.numpy as jnp
import numpy as np
from jax import lax
from jax.experimental import pallas as pl
from jax.experimental.pallas import tpu as pltpu
from jax.sharding import PartitionSpec as P

BF = jnp.bfloat16
F32 = jnp.float32
HALO = 16
DEEP = 14
LIMIT = 20
EDGE_CELLS = 2048
RSQRT2 = np.float32(0.7071067811865476)


def conv_norm(layer, shifted, width, base, chunks, w_ref, nrm):
    dil = 2 ** (layer + 1)
    weight = w_ref[layer].reshape(-1, w_ref.shape[-1])
    at = 0
    for first, count, turned in chunks:
        taps = [(a, b) for a in range(3) for b in range(3)]
        if turned:
            taps = taps[::-1]
        size = count * width
        lhs = jnp.concatenate(
            [
                shifted[b, (first - base + (a - 1) * dil) * width : (first - base + (a - 1) * dil) * width + size]
                for a, b in taps
            ],
            axis=1,
        )
        conv = jnp.dot(lhs, weight, preferred_element_type=F32)
        mean = jnp.mean(conv, axis=-1, keepdims=True)
        centred = conv - mean
        var = jnp.mean(centred * centred, axis=-1, keepdims=True)
        nrm[at : at + size] = (centred * lax.rsqrt(var + 1e-05)).astype(BF)
        at += size


def mlp(layer, shifted, width, base, first, counts, up_ref, down_ref, mask_ref, nrm, store, mask_base=0):
    at = 0
    row = first
    for count in counts:
        size = count * width
        pre = jnp.dot(nrm[at : at + size], up_ref[layer], preferred_element_type=F32)
        hidden = (0.5 * pre * (1.0 + lax.erf(pre * RSQRT2))).astype(BF)
        branch = jnp.dot(hidden, down_ref[layer], preferred_element_type=F32)
        centre = shifted[1, (row - base) * width : (row - base) * width + size].astype(F32)
        mask = mask_ref[(row - mask_base) * width : (row - mask_base) * width + size].astype(F32)
        mask = jnp.concatenate([mask, mask], axis=1)
        store(row, count, (mask * (centre + branch)).astype(BF))
        at += size
        row += count


def spread(shifted, at, values, starts, size, dil):
    for b in range(3):
        for k, start in enumerate(starts):
            lo = start + (b - 1) * dil
            shifted[b, at + k * size : at + (k + 1) * size] = values[lo : lo + size]


def clear(shifted, size):
    for b in range(3):
        shifted[b, :size] = jnp.zeros((size, shifted.shape[-1]), BF)


def keep(ref, width, base):
    def store(row, count, value):
        ref[(row - base) * width : (row - base + count) * width] = value

    return store


def diagonal(turned, size=64):
    rows = lax.broadcasted_iota(jnp.int32, (size, size), 0)
    cols = lax.broadcasted_iota(jnp.int32, (size, size), 1)
    return rows + cols == size - 1 if turned else rows == cols


def spread_mask(land, first, count, turned):
    lines = jnp.where(diagonal(turned)[None], land[first : first + count][:, None, :], 0.0).astype(BF)
    cells = jnp.dot(lines.reshape(count * 64, 64), jnp.ones((64, 128), BF), preferred_element_type=F32)
    return cells.astype(BF).reshape(count, 64, 128)


def window(whole, first):
    total = whole.shape[1]
    source = lax.broadcasted_iota(jnp.int32, (total, 64), 0)
    target = lax.broadcasted_iota(jnp.int32, (total, 64), 1) + first
    target = jnp.where(target < 0, target + total, target)
    target = jnp.where(target >= total, target - total, target)
    pick = jnp.where(source == target, 1.0, 0.0).astype(BF)
    return jnp.dot(whole, pick, preferred_element_type=F32)


def halves(value, inner, outer):
    odd = lax.rem(lax.axis_index("lon"), 2) == 1
    for row in range(value.shape[0]):
        low, high = value[row, 0:HALO], value[row, 32 - HALO : 32]
        inner[row] = jnp.where(odd, low, high)
        outer[row] = jnp.where(odd, high, low)


def edges_kernel(own, inner, outer, top):
    halves(own, inner, outer)
    top[...] = own[32 - DEEP : 32]


def cut_kernel(north, inner, outer):
    halves(north, outer, inner)


def in_order(row, inner, outer):
    odd = lax.rem(lax.axis_index("lon"), 2) == 1
    return jnp.where(odd, inner[row], outer[row]), jnp.where(odd, outer[row], inner[row])


def wide(row, inner, own, outer):
    before, after = in_order(row, inner, outer)
    return jnp.concatenate([before, own[row], after], axis=0)


def first_kernel(own, land_sea, w, up, down, x1, mask, land, land_north, sh1, nrm, m1):
    me = lax.axis_index("lon")
    whole = land_sea[...].astype(F32).astype(BF)
    land[...] = window(whole, me * 32 - HALO)
    land_north[...] = window(whole, (lax.axis_size("lon") - 1 - me) * 32 - HALO)[32 - DEEP :]
    cells = spread_mask(land, 0, 32, False)
    mask[...] = cells[:, 16:48].reshape(32 * 32, 128)
    m1[...] = cells[:30, 20:44].reshape(30 * 24, 128)
    clear(sh1, 2 * 24)
    for row in range(32):
        spread(sh1, (row + 2) * 24, own[row], [4], 24, 2)
    conv_norm(0, sh1, 24, -2, [(0, 8, False), (8, 8, False), (16, 8, False), (24, 6, False)], w, nrm)
    mlp(0, sh1, 24, -2, 0, [16, 14], up, down, m1, nrm, keep(x1, 24, 0))


def second_kernel(x1, mask, w, up, down, x2, sh2, nrm, m2):
    for row in range(26):
        m2[row * 16 : (row + 1) * 16] = mask[row * 32 + 8 : row * 32 + 24]
    clear(sh2, 4 * 16)
    for row in range(30):
        spread(sh2, (row + 4) * 16, x1[row * 24 : (row + 1) * 24], [4], 16, 4)
    conv_norm(1, sh2, 16, -4, [(0, 13, False), (13, 13, False)], w, nrm)
    mlp(1, sh2, 16, -4, 0, [26], up, down, m2, nrm, keep(x2, 16, 0))


def south_kernel(
    inner, own, outer, x1_mid, x2_mid, land, mask, w, up, down,
    x1_tail, x2_tail, out, sh1, sh2, sh3, x1, x2, nrm, e1, e2,
):
    clear(sh1, 2 * 32)
    clear(sh2, 4 * 32)
    clear(sh3, 8 * 32)
    for row in range(32):
        spread(sh1, (row + 2) * 32, wide(row, inner, own, outer), [4, 44], 16, 2)
    cells = spread_mask(land, 0, 30, False)
    e1[...] = jnp.concatenate([cells[:, 4:20], cells[:, 44:60]], axis=1).reshape(30 * 32, 128)
    e2[...] = jnp.concatenate([cells[:26, 8:24], cells[:26, 40:56]], axis=1).reshape(26 * 32, 128)
    conv_norm(0, sh1, 32, -2, [(0, 8, False), (8, 8, False), (16, 7, False), (23, 7, False)], w, nrm)
    mlp(0, sh1, 32, -2, 0, [15, 15], up, down, e1, nrm, keep(x1, 32, 0))

    def row1(row):
        at = row * 32
        return jnp.concatenate([x1[at : at + 16], x1_mid[row * 24 : (row + 1) * 24], x1[at + 16 : at + 32]], axis=0)

    for row in range(30):
        values = row1(row)
        if row >= 22:
            x1_tail[(row - 22) * 56 : (row - 21) * 56] = values
        spread(sh2, (row + 4) * 32, values, [4, 36], 16, 4)
    conv_norm(1, sh2, 32, -4, [(0, 7, False), (7, 7, False), (14, 6, False), (20, 6, False)], w, nrm)
    mlp(1, sh2, 32, -4, 0, [13, 13], up, down, e2, nrm, keep(x2, 32, 0))
    for row in range(26):
        at = row * 32
        values = jnp.concatenate([x2[at : at + 16], x2_mid[row * 16 : (row + 1) * 16], x2[at + 16 : at + 32]], axis=0)
        if row >= 10:
            x2_tail[(row - 10) * 48 : (row - 9) * 48] = values
        spread(sh3, (row + 8) * 32, values, [8], 32, 8)
    conv_norm(2, sh3, 32, -8, [(0, 6, False), (6, 6, False), (12, 6, False)], w, nrm)

    def store3(row, count, value):
        out[row : row + count] = value.reshape(count, 32, 256)

    mlp(2, sh3, 32, -8, 0, [9, 9], up, down, mask, nrm, store3)


def strips(cells, left, right):
    rows = cells.shape[0]
    return jnp.concatenate([cells[:, left : left + 16], cells[:, right : right + 16]], axis=1).reshape(rows * 32, 128)


def fold_kernel(own, north, x1_tail, land, land_north, w, up, down, x1, x2, e1, e2, sh1, sh2, nrm, m1, m2):
    near = spread_mask(land, 26, 6, False)
    far = spread_mask(land_north, 0, DEEP, True)
    cells = jnp.concatenate([near] + [far[45 - row : 46 - row] for row in range(32, 44)], axis=0)
    m1[...] = cells[4:, 20:44].reshape(14 * 24, 128)
    m2[...] = cells[:14, 24:40].reshape(14 * 16, 128)
    e1[...] = strips(cells[4:], 4, 44)
    e2[...] = strips(cells[:14], 8, 40)
    turn = jnp.where(diagonal(True, 32), 1.0, 0.0).astype(BF)
    for row in range(18):
        if row < 4:
            line = own[28 + row]
        else:
            line = jnp.dot(turn, north[17 - row], preferred_element_type=F32).astype(BF)
        spread(sh1, row * 24, line, [4], 24, 2)
    conv_norm(0, sh1, 24, 28, [(30, 2, False), (32, 6, True), (38, 6, True)], w, nrm)
    mlp(0, sh1, 24, 28, 30, [8, 6], up, down, m1, nrm, keep(x1, 24, 30), 30)
    for row in range(8):
        spread(sh2, row * 16, x1_tail[row * 56 : (row + 1) * 56], [20], 16, 4)
    for row in range(14):
        spread(sh2, (row + 8) * 16, x1[row * 24 : (row + 1) * 24], [4], 16, 4)
    conv_norm(1, sh2, 16, 22, [(26, 6, False), (32, 8, True)], w, nrm)
    mlp(1, sh2, 16, 22, 26, [7, 7], up, down, m2, nrm, keep(x2, 16, 26), 26)


def north_kernel(
    inner, own, outer, north, north_inner, north_outer, x1_tail, x2_tail, out_south, x1_mid, x2_mid,
    e1, e2, mask, w, up, down, out, sh1, sh2, sh3, x1, x2, nrm, last, sems,
):
    first = pltpu.make_async_copy(out_south, out.at[0:18], sems.at[0])
    first.start()
    half = lax.axis_size("lon") // 2
    place = lax.rem(lax.axis_index("lon"), half)
    turn = jnp.where(diagonal(True), 1.0, 0.0).astype(BF)
    for row in range(4):
        spread(sh1, row * 32, wide(28 + row, inner, own, outer), [4, 44], 16, 2)
    for row in range(14):
        at = 13 - row
        after, before = in_order(at, north_inner, north_outer)
        after = jnp.where(place == 0, own[18 + at, 0:HALO], after)
        before = jnp.where(place == half - 1, own[18 + at, 32 - HALO : 32], before)
        source = jnp.concatenate([before, north[at], after], axis=0)
        turned = jnp.dot(turn, source, preferred_element_type=F32).astype(BF)
        spread(sh1, (row + 4) * 32, turned, [4, 44], 16, 2)
    conv_norm(0, sh1, 32, 28, [(30, 2, False), (32, 6, True), (38, 6, True)], w, nrm)
    mlp(0, sh1, 32, 28, 30, [7, 7], up, down, e1, nrm, keep(x1, 32, 30), 30)
    for row in range(8):
        spread(sh2, row * 32, x1_tail[row * 56 : (row + 1) * 56], [4, 36], 16, 4)
    for row in range(14):
        at = row * 32
        values = jnp.concatenate([x1[at : at + 16], x1_mid[row * 24 : (row + 1) * 24], x1[at + 16 : at + 32]], axis=0)
        spread(sh2, (row + 8) * 32, values, [4, 36], 16, 4)
    conv_norm(1, sh2, 32, 22, [(26, 6, False), (32, 8, True)], w, nrm)
    mlp(1, sh2, 32, 22, 26, [7, 7], up, down, e2, nrm, keep(x2, 32, 26), 26)
    for row in range(16):
        spread(sh3, row * 32, x2_tail[row * 48 : (row + 1) * 48], [8], 32, 8)
    for row in range(14):
        at = row * 32
        values = jnp.concatenate([x2[at : at + 16], x2_mid[row * 16 : (row + 1) * 16], x2[at + 16 : at + 32]], axis=0)
        spread(sh3, (row + 16) * 32, values, [8], 32, 8)
    conv_norm(2, sh3, 32, 10, [(18, 7, False), (25, 7, False)], w, nrm)

    copies = [first]

    def store3(row, count, value):
        last[row - 18 : row - 18 + count] = value.reshape(count, 32, 256)
        here = pltpu.make_async_copy(
            last.at[row - 18 : row - 18 + count], out.at[row : row + count], sems.at[len(copies)]
        )
        here.start()
        copies.append(here)

    mlp(2, sh3, 32, 10, 18, [7, 7], up, down, mask, nrm, store3)
    for copy in copies:
        copy.wait()


def cost(cells):
    return pl.CostEstimate(
        flops=2 * cells * (9 * 256 * 256 + 2 * 256 * 1024), bytes_accessed=2**20, transcendentals=cells * 1024
    )


VMEM = pl.BlockSpec(memory_space=pltpu.VMEM)
HBM = pl.BlockSpec(memory_space=pltpu.HBM)


def call(kernel, name, outs, in_specs, out_specs, scratch, cells, args, limit=LIMIT):
    return pl.pallas_call(
        kernel,
        name=name,
        out_shape=tuple(jax.ShapeDtypeStruct(*(out if isinstance(out[0], tuple) else (out, BF))) for out in outs),
        in_specs=in_specs,
        out_specs=tuple(out_specs),
        scratch_shapes=scratch,
        compiler_params=pltpu.CompilerParams(vmem_limit_bytes=limit * 2**20),
        cost_estimate=cost(cells),
    )(*args)


def taps(rows, width):
    return pltpu.VMEM((3, rows * width, 256), BF)


def flat(rows, width):
    return pltpu.VMEM((rows * width, 256), BF)


def edges_call(own):
    return call(
        edges_kernel, "edges", [(32, HALO, 256), (32, HALO, 256), (DEEP, 32, 256)], [VMEM], [VMEM] * 3, [],
        EDGE_CELLS, (own,),
    )


def cut_call(north):
    return call(cut_kernel, "cut", [(DEEP, HALO, 256)] * 2, [VMEM], [VMEM] * 2, [], 0, (north,))


def first_call(*args):
    return call(
        first_kernel, "first", [(30 * 24, 256), (32 * 32, 128), ((32, 64), F32), ((DEEP, 64), F32)],
        [VMEM] * len(args), [VMEM] * 4,
        [taps(34, 24), flat(30, 24), pltpu.VMEM((30 * 24, 128), BF)], 720, args,
    )


def second_call(*args):
    (x2,) = call(
        second_kernel, "second", [(26 * 16, 256)], [VMEM] * len(args), [VMEM],
        [taps(34, 16), flat(26, 16), pltpu.VMEM((26 * 16, 128), BF)], 416, args,
    )
    return x2


def south_call(*args):
    return call(
        south_kernel, "south", [(8 * 56, 256), (16 * 48, 256), (18, 32, 256)], [VMEM] * len(args), [VMEM] * 3,
        [taps(34, 32), taps(34, 32), taps(34, 32), flat(30, 32), flat(26, 32), flat(30, 32),
         pltpu.VMEM((30 * 32, 128), BF), pltpu.VMEM((26 * 32, 128), BF)],
        2368, args,
    )


def fold_call(*args):
    return call(
        fold_kernel, "fold", [(14 * 24, 256), (14 * 16, 256), (14 * 32, 128), (14 * 32, 128)],
        [VMEM] * len(args), [VMEM] * 4,
        [taps(18, 24), taps(22, 16), flat(14, 24), pltpu.VMEM((14 * 24, 128), BF), pltpu.VMEM((14 * 16, 128), BF)],
        560, args,
    )


def north_call(*args):
    (out,) = call(
        north_kernel, "north", [(32, 32, 256)], [VMEM] * len(args), [HBM],
        [
            taps(18, 32), taps(22, 32), taps(30, 32), flat(14, 32), flat(14, 32), flat(14, 32),
            pltpu.VMEM((14, 32, 256), BF), pltpu.SemaphoreType.DMA((3,)),
        ],
        1344, args,
    )
    return out


def swap_inner(value):
    return lax.ppermute(value, "lon", [(i, i ^ 1) for i in range(lax.axis_size("lon"))])


def swap_outer(value, ring=1):
    count = lax.axis_size("lon") // ring
    return lax.ppermute(
        value, "lon", [(i, i // count * count + (((i + 1) ^ 1) - 1) % count) for i in range(ring * count)]
    )


def per_device(own, land_sea, w, up, down):
    count = lax.axis_size("lon")
    cols = own.shape[1]
    to_inner, to_outer, top = edges_call(own)
    inner = swap_inner(to_inner)
    outer = swap_outer(to_outer)
    weights = (w, up, down)
    x1_mid, mask, land, land_north = first_call(own, land_sea, *weights)
    top, x1_mid = lax.optimization_barrier((top, x1_mid))
    north = lax.ppermute(top, "lon", [(i, count - 1 - i) for i in range(count)])
    x2_mid = second_call(x1_mid, mask, *weights)
    x1_tail, x2_tail, out_south = south_call(inner, own, outer, x1_mid, x2_mid, land, mask, *weights)
    north, x1_tail = lax.optimization_barrier((north, x1_tail))
    to_inner, to_outer = cut_call(north)
    north_inner = swap_inner(to_inner)
    north_outer = swap_outer(to_outer, 2)
    y1_mid, y2_mid, e1, e2 = fold_call(own, north, x1_tail, land, land_north, *weights)
    return north_call(
        inner, own, outer, north, north_inner, north_outer, x1_tail, x2_tail, out_south, y1_mid, y2_mid, e1, e2, mask, *weights
    )


def solution(mesh):
    in_specs = (P("parts", "lon", None), P(), P(), P(), P())
    out_specs = P("parts", "lon", None)
    return jax.shard_map(
        per_device, mesh=mesh, in_specs=in_specs, out_specs=out_specs, check_vma=False
    )
```

```python
import functools

import jax
import jax.numpy as jnp
import numpy as np
from jax import lax
from jax.experimental import pallas as pl
from jax.experimental.pallas import tpu as pltpu
from jax.sharding import PartitionSpec as P

BF = jnp.bfloat16
F32 = jnp.float32
HALO = 16
DEEP = 14
LIMIT = 20
EDGE_CELLS = 2048
RSQRT2 = np.float32(0.7071067811865476)


def conv_norm(layer, shifted, width, base, chunks, w_ref, nrm):
    dil = 2 ** (layer + 1)
    weight = w_ref[layer].reshape(-1, w_ref.shape[-1])
    at = 0
    for first, count, turned in chunks:
        taps = [(a, b) for a in range(3) for b in range(3)]
        if turned:
            taps = taps[::-1]
        size = count * width
        lhs = jnp.concatenate(
            [
                shifted[b, (first - base + (a - 1) * dil) * width : (first - base + (a - 1) * dil) * width + size]
                for a, b in taps
            ],
            axis=1,
        )
        conv = jnp.dot(lhs, weight, preferred_element_type=F32)
        mean = jnp.mean(conv, axis=-1, keepdims=True)
        centred = conv - mean
        var = jnp.mean(centred * centred, axis=-1, keepdims=True)
        nrm[at : at + size] = (centred * lax.rsqrt(var + 1e-05)).astype(BF)
        at += size


def mlp(layer, shifted, width, base, first, counts, up_ref, down_ref, mask_ref, nrm, store, mask_base=0):
    at = 0
    row = first
    for count in counts:
        size = count * width
        pre = jnp.dot(nrm[at : at + size], up_ref[layer], preferred_element_type=F32)
        hidden = (0.5 * pre * (1.0 + lax.erf(pre * RSQRT2))).astype(BF)
        branch = jnp.dot(hidden, down_ref[layer], preferred_element_type=F32)
        centre = shifted[1, (row - base) * width : (row - base) * width + size].astype(F32)
        mask = mask_ref[(row - mask_base) * width : (row - mask_base) * width + size].astype(F32)
        mask = jnp.concatenate([mask, mask], axis=1)
        store(row, count, (mask * (centre + branch)).astype(BF))
        at += size
        row += count


def spread(shifted, at, values, starts, size, dil):
    for b in range(3):
        for k, start in enumerate(starts):
            lo = start + (b - 1) * dil
            shifted[b, at + k * size : at + (k + 1) * size] = values[lo : lo + size]


def clear(shifted, size):
    for b in range(3):
        shifted[b, :size] = jnp.zeros((size, shifted.shape[-1]), BF)


def keep(ref, width, base):
    def store(row, count, value):
        ref[(row - base) * width : (row - base + count) * width] = value

    return store


def diagonal(turned, size=64):
    rows = lax.broadcasted_iota(jnp.int32, (size, size), 0)
    cols = lax.broadcasted_iota(jnp.int32, (size, size), 1)
    return rows + cols == size - 1 if turned else rows == cols


def spread_mask(land, first, count, turned):
    lines = jnp.where(diagonal(turned)[None], land[first : first + count][:, None, :], 0.0).astype(BF)
    cells = jnp.dot(lines.reshape(count * 64, 64), jnp.ones((64, 128), BF), preferred_element_type=F32)
    return cells.astype(BF).reshape(count, 64, 128)


def window(whole, first):
    total = whole.shape[1]
    source = lax.broadcasted_iota(jnp.int32, (total, 64), 0)
    target = lax.broadcasted_iota(jnp.int32, (total, 64), 1) + first
    target = jnp.where(target < 0, target + total, target)
    target = jnp.where(target >= total, target - total, target)
    pick = jnp.where(source == target, 1.0, 0.0).astype(BF)
    return jnp.dot(whole, pick, preferred_element_type=F32)


def halves(value, inner, outer):
    odd = lax.rem(lax.axis_index("lon"), 2) == 1
    for row in range(value.shape[0]):
        low, high = value[row, 0:HALO], value[row, 32 - HALO : 32]
        inner[row] = jnp.where(odd, low, high)
        outer[row] = jnp.where(odd, high, low)


def edges_kernel(own, inner, outer, top):
    halves(own, inner, outer)
    top[...] = own[32 - DEEP : 32]


def cut_kernel(north, inner, outer):
    halves(north, outer, inner)


def in_order(row, inner, outer):
    odd = lax.rem(lax.axis_index("lon"), 2) == 1
    return jnp.where(odd, inner[row], outer[row]), jnp.where(odd, outer[row], inner[row])


def wide(row, inner, own, outer):
    before, after = in_order(row, inner, outer)
    return jnp.concatenate([before, own[row], after], axis=0)


def first_kernel(own, land_sea, w, up, down, x1, mask, land, land_north, sh1, nrm, m1):
    me = lax.axis_index("lon")
    whole = land_sea[...].astype(F32).astype(BF)
    land[...] = window(whole, me * 32 - HALO)
    land_north[...] = window(whole, (lax.axis_size("lon") - 1 - me) * 32 - HALO)[32 - DEEP :]
    cells = spread_mask(land, 0, 32, False)
    mask[...] = cells[:, 16:48].reshape(32 * 32, 128)
    m1[...] = cells[:30, 20:44].reshape(30 * 24, 128)
    clear(sh1, 2 * 24)
    for row in range(32):
        spread(sh1, (row + 2) * 24, own[row], [4], 24, 2)
    conv_norm(0, sh1, 24, -2, [(0, 8, False), (8, 8, False), (16, 8, False), (24, 6, False)], w, nrm)
    mlp(0, sh1, 24, -2, 0, [10, 10, 10], up, down, m1, nrm, keep(x1, 24, 0))


def second_kernel(x1, mask, w, up, down, x2, sh2, nrm, m2):
    for row in range(26):
        m2[row * 16 : (row + 1) * 16] = mask[row * 32 + 8 : row * 32 + 24]
    clear(sh2, 4 * 16)
    for row in range(30):
        spread(sh2, (row + 4) * 16, x1[row * 24 : (row + 1) * 24], [4], 16, 4)
    conv_norm(1, sh2, 16, -4, [(0, 13, False), (13, 13, False)], w, nrm)
    mlp(1, sh2, 16, -4, 0, [13, 13], up, down, m2, nrm, keep(x2, 16, 0))


def south_kernel(
    inner, own, outer, x1_mid, x2_mid, land, mask, w, up, down,
    x1_tail, x2_tail, out, sh1, sh2, sh3, x1, x2, nrm, e1, e2,
):
    clear(sh1, 2 * 32)
    clear(sh2, 4 * 32)
    clear(sh3, 8 * 32)
    for row in range(32):
        spread(sh1, (row + 2) * 32, wide(row, inner, own, outer), [4, 44], 16, 2)
    cells = spread_mask(land, 0, 30, False)
    e1[...] = jnp.concatenate([cells[:, 4:20], cells[:, 44:60]], axis=1).reshape(30 * 32, 128)
    e2[...] = jnp.concatenate([cells[:26, 8:24], cells[:26, 40:56]], axis=1).reshape(26 * 32, 128)
    conv_norm(0, sh1, 32, -2, [(0, 8, False), (8, 8, False), (16, 7, False), (23, 7, False)], w, nrm)
    mlp(0, sh1, 32, -2, 0, [15, 15], up, down, e1, nrm, keep(x1, 32, 0))

    def row1(row):
        at = row * 32
        return jnp.concatenate([x1[at : at + 16], x1_mid[row * 24 : (row + 1) * 24], x1[at + 16 : at + 32]], axis=0)

    for row in range(30):
        values = row1(row)
        if row >= 22:
            x1_tail[(row - 22) * 56 : (row - 21) * 56] = values
        spread(sh2, (row + 4) * 32, values, [4, 36], 16, 4)
    conv_norm(1, sh2, 32, -4, [(0, 7, False), (7, 7, False), (14, 6, False), (20, 6, False)], w, nrm)
    mlp(1, sh2, 32, -4, 0, [13, 13], up, down, e2, nrm, keep(x2, 32, 0))
    for row in range(26):
        at = row * 32
        values = jnp.concatenate([x2[at : at + 16], x2_mid[row * 16 : (row + 1) * 16], x2[at + 16 : at + 32]], axis=0)
        if row >= 10:
            x2_tail[(row - 10) * 48 : (row - 9) * 48] = values
        spread(sh3, (row + 8) * 32, values, [8], 32, 8)
    conv_norm(2, sh3, 32, -8, [(0, 6, False), (6, 6, False), (12, 6, False)], w, nrm)

    def store3(row, count, value):
        out[row : row + count] = value.reshape(count, 32, 256)

    mlp(2, sh3, 32, -8, 0, [9, 9], up, down, mask, nrm, store3)


def strips(cells, left, right):
    rows = cells.shape[0]
    return jnp.concatenate([cells[:, left : left + 16], cells[:, right : right + 16]], axis=1).reshape(rows * 32, 128)


def fold_kernel(own, north, x1_tail, land, land_north, w, up, down, x1, x2, e1, e2, sh1, sh2, nrm, m1, m2):
    near = spread_mask(land, 26, 6, False)
    far = spread_mask(land_north, 0, DEEP, True)
    cells = jnp.concatenate([near] + [far[45 - row : 46 - row] for row in range(32, 44)], axis=0)
    m1[...] = cells[4:, 20:44].reshape(14 * 24, 128)
    m2[...] = cells[:14, 24:40].reshape(14 * 16, 128)
    e1[...] = strips(cells[4:], 4, 44)
    e2[...] = strips(cells[:14], 8, 40)
    turn = jnp.where(diagonal(True, 32), 1.0, 0.0).astype(BF)
    for row in range(18):
        if row < 4:
            line = own[28 + row]
        else:
            line = jnp.dot(turn, north[17 - row], preferred_element_type=F32).astype(BF)
        spread(sh1, row * 24, line, [4], 24, 2)
    conv_norm(0, sh1, 24, 28, [(30, 2, False), (32, 6, True), (38, 6, True)], w, nrm)
    mlp(0, sh1, 24, 28, 30, [8, 6], up, down, m1, nrm, keep(x1, 24, 30), 30)
    for row in range(8):
        spread(sh2, row * 16, x1_tail[row * 56 : (row + 1) * 56], [20], 16, 4)
    for row in range(14):
        spread(sh2, (row + 8) * 16, x1[row * 24 : (row + 1) * 24], [4], 16, 4)
    conv_norm(1, sh2, 16, 22, [(26, 6, False), (32, 8, True)], w, nrm)
    mlp(1, sh2, 16, 22, 26, [7, 7], up, down, m2, nrm, keep(x2, 16, 26), 26)


def north_kernel(
    inner, own, outer, north, north_inner, north_outer, x1_tail, x2_tail, out_south, x1_mid, x2_mid,
    e1, e2, mask, w, up, down, out, sh1, sh2, sh3, x1, x2, nrm, last, sems,
):
    first = pltpu.make_async_copy(out_south, out.at[0:18], sems.at[0])
    first.start()
    half = lax.axis_size("lon") // 2
    place = lax.rem(lax.axis_index("lon"), half)
    turn = jnp.where(diagonal(True), 1.0, 0.0).astype(BF)
    for row in range(4):
        spread(sh1, row * 32, wide(28 + row, inner, own, outer), [4, 44], 16, 2)
    for row in range(14):
        at = 13 - row
        after, before = in_order(at, north_inner, north_outer)
        after = jnp.where(place == 0, own[18 + at, 0:HALO], after)
        before = jnp.where(place == half - 1, own[18 + at, 32 - HALO : 32], before)
        source = jnp.concatenate([before, north[at], after], axis=0)
        turned = jnp.dot(turn, source, preferred_element_type=F32).astype(BF)
        spread(sh1, (row + 4) * 32, turned, [4, 44], 16, 2)
    conv_norm(0, sh1, 32, 28, [(30, 2, False), (32, 6, True), (38, 6, True)], w, nrm)
    mlp(0, sh1, 32, 28, 30, [7, 7], up, down, e1, nrm, keep(x1, 32, 30), 30)
    for row in range(8):
        spread(sh2, row * 32, x1_tail[row * 56 : (row + 1) * 56], [4, 36], 16, 4)
    for row in range(14):
        at = row * 32
        values = jnp.concatenate([x1[at : at + 16], x1_mid[row * 24 : (row + 1) * 24], x1[at + 16 : at + 32]], axis=0)
        spread(sh2, (row + 8) * 32, values, [4, 36], 16, 4)
    conv_norm(1, sh2, 32, 22, [(26, 6, False), (32, 4, True), (36, 4, True)], w, nrm)
    mlp(1, sh2, 32, 22, 26, [7, 7], up, down, e2, nrm, keep(x2, 32, 26), 26)
    for row in range(16):
        spread(sh3, row * 32, x2_tail[row * 48 : (row + 1) * 48], [8], 32, 8)
    for row in range(14):
        at = row * 32
        values = jnp.concatenate([x2[at : at + 16], x2_mid[row * 16 : (row + 1) * 16], x2[at + 16 : at + 32]], axis=0)
        spread(sh3, (row + 16) * 32, values, [8], 32, 8)
    conv_norm(2, sh3, 32, 10, [(18, 7, False), (25, 7, False)], w, nrm)

    copies = [first]

    def store3(row, count, value):
        last[row - 18 : row - 18 + count] = value.reshape(count, 32, 256)
        here = pltpu.make_async_copy(
            last.at[row - 18 : row - 18 + count], out.at[row : row + count], sems.at[len(copies)]
        )
        here.start()
        copies.append(here)

    mlp(2, sh3, 32, 10, 18, [7, 7], up, down, mask, nrm, store3)
    for copy in copies:
        copy.wait()


def cost(cells):
    return pl.CostEstimate(
        flops=2 * cells * (9 * 256 * 256 + 2 * 256 * 1024), bytes_accessed=2**20, transcendentals=cells * 1024
    )


VMEM = pl.BlockSpec(memory_space=pltpu.VMEM)
HBM = pl.BlockSpec(memory_space=pltpu.HBM)


def call(kernel, name, outs, in_specs, out_specs, scratch, cells, args, limit=LIMIT):
    return pl.pallas_call(
        kernel,
        name=name,
        out_shape=tuple(jax.ShapeDtypeStruct(*(out if isinstance(out[0], tuple) else (out, BF))) for out in outs),
        in_specs=in_specs,
        out_specs=tuple(out_specs),
        scratch_shapes=scratch,
        compiler_params=pltpu.CompilerParams(vmem_limit_bytes=limit * 2**20),
        cost_estimate=cost(cells),
    )(*args)


def taps(rows, width):
    return pltpu.VMEM((3, rows * width, 256), BF)


def flat(rows, width):
    return pltpu.VMEM((rows * width, 256), BF)


def edges_call(own):
    return call(
        edges_kernel, "edges", [(32, HALO, 256), (32, HALO, 256), (DEEP, 32, 256)], [VMEM], [VMEM] * 3, [],
        EDGE_CELLS, (own,),
    )


def cut_call(north):
    return call(cut_kernel, "cut", [(DEEP, HALO, 256)] * 2, [VMEM], [VMEM] * 2, [], 0, (north,))


def first_call(*args):
    return call(
        first_kernel, "first", [(30 * 24, 256), (32 * 32, 128), ((32, 64), F32), ((DEEP, 64), F32)],
        [VMEM] * len(args), [VMEM] * 4,
        [taps(34, 24), flat(30, 24), pltpu.VMEM((30 * 24, 128), BF)], 720, args,
    )


def second_call(*args):
    (x2,) = call(
        second_kernel, "second", [(26 * 16, 256)], [VMEM] * len(args), [VMEM],
        [taps(34, 16), flat(26, 16), pltpu.VMEM((26 * 16, 128), BF)], 416, args,
    )
    return x2


def south_call(*args):
    return call(
        south_kernel, "south", [(8 * 56, 256), (16 * 48, 256), (18, 32, 256)], [VMEM] * len(args), [VMEM] * 3,
        [taps(34, 32), taps(34, 32), taps(34, 32), flat(30, 32), flat(26, 32), flat(30, 32),
         pltpu.VMEM((30 * 32, 128), BF), pltpu.VMEM((26 * 32, 128), BF)],
        2368, args,
    )


def fold_call(*args):
    return call(
        fold_kernel, "fold", [(14 * 24, 256), (14 * 16, 256), (14 * 32, 128), (14 * 32, 128)],
        [VMEM] * len(args), [VMEM] * 4,
        [taps(18, 24), taps(22, 16), flat(14, 24), pltpu.VMEM((14 * 24, 128), BF), pltpu.VMEM((14 * 16, 128), BF)],
        560, args,
    )


def north_call(*args):
    (out,) = call(
        north_kernel, "north", [(32, 32, 256)], [VMEM] * len(args), [HBM],
        [
            taps(18, 32), taps(22, 32), taps(30, 32), flat(14, 32), flat(14, 32), flat(14, 32),
            pltpu.VMEM((14, 32, 256), BF), pltpu.SemaphoreType.DMA((3,)),
        ],
        1344, args,
    )
    return out


def swap_inner(value):
    return lax.ppermute(value, "lon", [(i, i ^ 1) for i in range(lax.axis_size("lon"))])


def swap_outer(value, ring=1):
    count = lax.axis_size("lon") // ring
    return lax.ppermute(
        value, "lon", [(i, i // count * count + (((i + 1) ^ 1) - 1) % count) for i in range(ring * count)]
    )


def per_device(own, land_sea, w, up, down):
    count = lax.axis_size("lon")
    cols = own.shape[1]
    to_inner, to_outer, top = edges_call(own)
    inner = swap_inner(to_inner)
    outer = swap_outer(to_outer)
    weights = (w, up, down)
    x1_mid, mask, land, land_north = first_call(own, land_sea, *weights)
    top, x1_mid = lax.optimization_barrier((top, x1_mid))
    north = lax.ppermute(top, "lon", [(i, count - 1 - i) for i in range(count)])
    x2_mid = second_call(x1_mid, mask, *weights)
    x1_tail, x2_tail, out_south = south_call(inner, own, outer, x1_mid, x2_mid, land, mask, *weights)
    north, x1_tail = lax.optimization_barrier((north, x1_tail))
    to_inner, to_outer = cut_call(north)
    north_inner = swap_inner(to_inner)
    north_outer = swap_outer(to_outer, 2)
    y1_mid, y2_mid, e1, e2 = fold_call(own, north, x1_tail, land, land_north, *weights)
    return north_call(
        inner, own, outer, north, north_inner, north_outer, x1_tail, x2_tail, out_south, y1_mid, y2_mid, e1, e2, mask, *weights
    )


def solution(mesh):
    in_specs = (P("parts", "lon", None), P(), P(), P(), P())
    out_specs = P("parts", "lon", None)
    return jax.shard_map(
        per_device, mesh=mesh, in_specs=in_specs, out_specs=out_specs, check_vma=False
    )
```

```python
import functools

import jax
import jax.numpy as jnp
import numpy as np
from jax import lax
from jax.experimental import pallas as pl
from jax.experimental.pallas import tpu as pltpu
from jax.sharding import PartitionSpec as P

BF = jnp.bfloat16
F32 = jnp.float32
HALO = 16
DEEP = 14
LIMIT = 20
EDGE_CELLS = 2048
RSQRT2 = np.float32(0.7071067811865476)


def conv_norm(layer, shifted, width, base, chunks, w_ref, nrm):
    dil = 2 ** (layer + 1)
    weight = w_ref[layer].reshape(-1, w_ref.shape[-1])
    at = 0
    for first, count, turned in chunks:
        taps = [(a, b) for a in range(3) for b in range(3)]
        if turned:
            taps = taps[::-1]
        size = count * width
        lhs = jnp.concatenate(
            [
                shifted[b, (first - base + (a - 1) * dil) * width : (first - base + (a - 1) * dil) * width + size]
                for a, b in taps
            ],
            axis=1,
        )
        conv = jnp.dot(lhs, weight, preferred_element_type=F32)
        mean = jnp.mean(conv, axis=-1, keepdims=True)
        centred = conv - mean
        var = jnp.mean(centred * centred, axis=-1, keepdims=True)
        nrm[at : at + size] = (centred * lax.rsqrt(var + 1e-05)).astype(BF)
        at += size


def mlp(layer, shifted, width, base, first, counts, up_ref, down_ref, mask_ref, nrm, store, mask_base=0):
    at = 0
    row = first
    for count in counts:
        size = count * width
        pre = jnp.dot(nrm[at : at + size], up_ref[layer], preferred_element_type=F32)
        hidden = (0.5 * pre * (1.0 + lax.erf(pre * RSQRT2))).astype(BF)
        branch = jnp.dot(hidden, down_ref[layer], preferred_element_type=F32)
        centre = shifted[1, (row - base) * width : (row - base) * width + size].astype(F32)
        value = centre + branch
        if mask_ref is not None:
            mask = mask_ref[(row - mask_base) * width : (row - mask_base) * width + size].astype(F32)
            value = jnp.concatenate([mask, mask], axis=1) * value
        store(row, count, value.astype(BF))
        at += size
        row += count


def spread(shifted, at, values, starts, size, dil):
    for b in range(3):
        for k, start in enumerate(starts):
            lo = start + (b - 1) * dil
            shifted[b, at + k * size : at + (k + 1) * size] = values[lo : lo + size]


def clear(shifted, size):
    for b in range(3):
        shifted[b, :size] = jnp.zeros((size, shifted.shape[-1]), BF)


def keep(ref, width, base):
    def store(row, count, value):
        ref[(row - base) * width : (row - base + count) * width] = value

    return store


def diagonal(turned, size=64):
    rows = lax.broadcasted_iota(jnp.int32, (size, size), 0)
    cols = lax.broadcasted_iota(jnp.int32, (size, size), 1)
    return rows + cols == size - 1 if turned else rows == cols


def spread_mask(land, first, count, turned):
    lines = jnp.where(diagonal(turned)[None], land[first : first + count][:, None, :], 0.0).astype(BF)
    cells = jnp.dot(lines.reshape(count * 64, 64), jnp.ones((64, 128), BF), preferred_element_type=F32)
    return cells.astype(BF).reshape(count, 64, 128)


def window(whole, first):
    total = whole.shape[1]
    source = lax.broadcasted_iota(jnp.int32, (total, 64), 0)
    target = lax.broadcasted_iota(jnp.int32, (total, 64), 1) + first
    target = jnp.where(target < 0, target + total, target)
    target = jnp.where(target >= total, target - total, target)
    pick = jnp.where(source == target, 1.0, 0.0).astype(BF)
    return jnp.dot(whole, pick, preferred_element_type=F32)


def halves(value, inner, outer):
    odd = lax.rem(lax.axis_index("lon"), 2) == 1
    for row in range(value.shape[0]):
        low, high = value[row, 0:HALO], value[row, 32 - HALO : 32]
        inner[row] = jnp.where(odd, low, high)
        outer[row] = jnp.where(odd, high, low)


def edges_kernel(own, inner, outer, top):
    halves(own, inner, outer)
    top[...] = own[32 - DEEP : 32]


def cut_kernel(north, inner, outer):
    halves(north, outer, inner)


def in_order(row, inner, outer):
    odd = lax.rem(lax.axis_index("lon"), 2) == 1
    return jnp.where(odd, inner[row], outer[row]), jnp.where(odd, outer[row], inner[row])


def wide(row, inner, own, outer):
    before, after = in_order(row, inner, outer)
    return jnp.concatenate([before, own[row], after], axis=0)


def first_kernel(own, w, up, down, x1, sh1, nrm):
    clear(sh1, 2 * 24)
    for row in range(32):
        spread(sh1, (row + 2) * 24, own[row], [4], 24, 2)
    conv_norm(0, sh1, 24, -2, [(0, 8, False), (8, 8, False), (16, 8, False), (24, 6, False)], w, nrm)
    mlp(0, sh1, 24, -2, 0, [10, 10, 10], up, down, None, nrm, keep(x1, 24, 0))


def second_kernel(raw, land_sea, w, up, down, x1, x2, mask, land, land_north, sh2, nrm, m2):
    me = lax.axis_index("lon")
    whole = land_sea[...].astype(F32).astype(BF)
    land[...] = window(whole, me * 32 - HALO)
    land_north[...] = window(whole, (lax.axis_size("lon") - 1 - me) * 32 - HALO)[32 - DEEP :]
    cells = spread_mask(land, 0, 32, False)
    mask[...] = cells[:, 16:48].reshape(32 * 32, 128)
    m2[...] = cells[:26, 24:40].reshape(26 * 16, 128)
    line = cells[:30, 20:44].reshape(30 * 24, 128)
    x1[...] = raw[...] * jnp.concatenate([line, line], axis=1)
    clear(sh2, 4 * 16)
    for row in range(30):
        spread(sh2, (row + 4) * 16, x1[row * 24 : (row + 1) * 24], [4], 16, 4)
    conv_norm(1, sh2, 16, -4, [(0, 13, False), (13, 13, False)], w, nrm)
    mlp(1, sh2, 16, -4, 0, [13, 13], up, down, m2, nrm, keep(x2, 16, 0))


def south_kernel(
    inner, own, outer, x1_mid, x2_mid, land, mask, w, up, down,
    x1_tail, x2_tail, out, sh1, sh2, sh3, x1, x2, nrm, e1, e2,
):
    clear(sh1, 2 * 32)
    clear(sh2, 4 * 32)
    clear(sh3, 8 * 32)
    for row in range(32):
        spread(sh1, (row + 2) * 32, wide(row, inner, own, outer), [4, 44], 16, 2)
    cells = spread_mask(land, 0, 30, False)
    e1[...] = jnp.concatenate([cells[:, 4:20], cells[:, 44:60]], axis=1).reshape(30 * 32, 128)
    e2[...] = jnp.concatenate([cells[:26, 8:24], cells[:26, 40:56]], axis=1).reshape(26 * 32, 128)
    conv_norm(0, sh1, 32, -2, [(0, 8, False), (8, 8, False), (16, 7, False), (23, 7, False)], w, nrm)
    mlp(0, sh1, 32, -2, 0, [15, 15], up, down, e1, nrm, keep(x1, 32, 0))

    def row1(row):
        at = row * 32
        return jnp.concatenate([x1[at : at + 16], x1_mid[row * 24 : (row + 1) * 24], x1[at + 16 : at + 32]], axis=0)

    for row in range(30):
        values = row1(row)
        if row >= 22:
            x1_tail[(row - 22) * 56 : (row - 21) * 56] = values
        spread(sh2, (row + 4) * 32, values, [4, 36], 16, 4)
    conv_norm(1, sh2, 32, -4, [(0, 7, False), (7, 7, False), (14, 6, False), (20, 6, False)], w, nrm)
    mlp(1, sh2, 32, -4, 0, [13, 13], up, down, e2, nrm, keep(x2, 32, 0))
    for row in range(26):
        at = row * 32
        values = jnp.concatenate([x2[at : at + 16], x2_mid[row * 16 : (row + 1) * 16], x2[at + 16 : at + 32]], axis=0)
        if row >= 10:
            x2_tail[(row - 10) * 48 : (row - 9) * 48] = values
        spread(sh3, (row + 8) * 32, values, [8], 32, 8)
    conv_norm(2, sh3, 32, -8, [(0, 6, False), (6, 6, False), (12, 6, False)], w, nrm)

    def store3(row, count, value):
        out[row : row + count] = value.reshape(count, 32, 256)

    mlp(2, sh3, 32, -8, 0, [9, 9], up, down, mask, nrm, store3)


def strips(cells, left, right):
    rows = cells.shape[0]
    return jnp.concatenate([cells[:, left : left + 16], cells[:, right : right + 16]], axis=1).reshape(rows * 32, 128)


def fold_kernel(own, north, x1_tail, land, land_north, w, up, down, x1, x2, e1, e2, sh1, sh2, nrm, m1, m2):
    near = spread_mask(land, 26, 6, False)
    far = spread_mask(land_north, 0, DEEP, True)
    cells = jnp.concatenate([near] + [far[45 - row : 46 - row] for row in range(32, 44)], axis=0)
    m1[...] = cells[4:, 20:44].reshape(14 * 24, 128)
    m2[...] = cells[:14, 24:40].reshape(14 * 16, 128)
    e1[...] = strips(cells[4:], 4, 44)
    e2[...] = strips(cells[:14], 8, 40)
    turn = jnp.where(diagonal(True, 32), 1.0, 0.0).astype(BF)
    for row in range(18):
        if row < 4:
            line = own[28 + row]
        else:
            line = jnp.dot(turn, north[17 - row], preferred_element_type=F32).astype(BF)
        spread(sh1, row * 24, line, [4], 24, 2)
    conv_norm(0, sh1, 24, 28, [(30, 2, False), (32, 6, True), (38, 6, True)], w, nrm)
    mlp(0, sh1, 24, 28, 30, [8, 6], up, down, m1, nrm, keep(x1, 24, 30), 30)
    for row in range(8):
        spread(sh2, row * 16, x1_tail[row * 56 : (row + 1) * 56], [20], 16, 4)
    for row in range(14):
        spread(sh2, (row + 8) * 16, x1[row * 24 : (row + 1) * 24], [4], 16, 4)
    conv_norm(1, sh2, 16, 22, [(26, 6, False), (32, 8, True)], w, nrm)
    mlp(1, sh2, 16, 22, 26, [7, 7], up, down, m2, nrm, keep(x2, 16, 26), 26)


def north_kernel(
    inner, own, outer, north, north_inner, north_outer, x1_tail, x2_tail, out_south, x1_mid, x2_mid,
    e1, e2, mask, w, up, down, out, sh1, sh2, sh3, x1, x2, nrm, last, sems,
):
    first = pltpu.make_async_copy(out_south, out.at[0:18], sems.at[0])
    first.start()
    half = lax.axis_size("lon") // 2
    place = lax.rem(lax.axis_index("lon"), half)
    turn = jnp.where(diagonal(True), 1.0, 0.0).astype(BF)
    for row in range(4):
        spread(sh1, row * 32, wide(28 + row, inner, own, outer), [4, 44], 16, 2)
    for row in range(14):
        at = 13 - row
        after, before = in_order(at, north_inner, north_outer)
        after = jnp.where(place == 0, own[18 + at, 0:HALO], after)
        before = jnp.where(place == half - 1, own[18 + at, 32 - HALO : 32], before)
        source = jnp.concatenate([before, north[at], after], axis=0)
        turned = jnp.dot(turn, source, preferred_element_type=F32).astype(BF)
        spread(sh1, (row + 4) * 32, turned, [4, 44], 16, 2)
    conv_norm(0, sh1, 32, 28, [(30, 2, False), (32, 6, True), (38, 6, True)], w, nrm)
    mlp(0, sh1, 32, 28, 30, [7, 7], up, down, e1, nrm, keep(x1, 32, 30), 30)
    for row in range(8):
        spread(sh2, row * 32, x1_tail[row * 56 : (row + 1) * 56], [4, 36], 16, 4)
    for row in range(14):
        at = row * 32
        values = jnp.concatenate([x1[at : at + 16], x1_mid[row * 24 : (row + 1) * 24], x1[at + 16 : at + 32]], axis=0)
        spread(sh2, (row + 8) * 32, values, [4, 36], 16, 4)
    conv_norm(1, sh2, 32, 22, [(26, 6, False), (32, 4, True), (36, 4, True)], w, nrm)
    mlp(1, sh2, 32, 22, 26, [7, 7], up, down, e2, nrm, keep(x2, 32, 26), 26)
    for row in range(16):
        spread(sh3, row * 32, x2_tail[row * 48 : (row + 1) * 48], [8], 32, 8)
    for row in range(14):
        at = row * 32
        values = jnp.concatenate([x2[at : at + 16], x2_mid[row * 16 : (row + 1) * 16], x2[at + 16 : at + 32]], axis=0)
        spread(sh3, (row + 16) * 32, values, [8], 32, 8)
    conv_norm(2, sh3, 32, 10, [(18, 7, False), (25, 7, False)], w, nrm)

    copies = [first]

    def store3(row, count, value):
        last[row - 18 : row - 18 + count] = value.reshape(count, 32, 256)
        here = pltpu.make_async_copy(
            last.at[row - 18 : row - 18 + count], out.at[row : row + count], sems.at[len(copies)]
        )
        here.start()
        copies.append(here)

    mlp(2, sh3, 32, 10, 18, [7, 7], up, down, mask, nrm, store3)
    for copy in copies:
        copy.wait()


def cost(cells):
    return pl.CostEstimate(
        flops=2 * cells * (9 * 256 * 256 + 2 * 256 * 1024), bytes_accessed=2**20, transcendentals=cells * 1024
    )


VMEM = pl.BlockSpec(memory_space=pltpu.VMEM)
HBM = pl.BlockSpec(memory_space=pltpu.HBM)


def call(kernel, name, outs, in_specs, out_specs, scratch, cells, args, limit=LIMIT):
    return pl.pallas_call(
        kernel,
        name=name,
        out_shape=tuple(jax.ShapeDtypeStruct(*(out if isinstance(out[0], tuple) else (out, BF))) for out in outs),
        in_specs=in_specs,
        out_specs=tuple(out_specs),
        scratch_shapes=scratch,
        compiler_params=pltpu.CompilerParams(vmem_limit_bytes=limit * 2**20),
        cost_estimate=cost(cells),
    )(*args)


def taps(rows, width):
    return pltpu.VMEM((3, rows * width, 256), BF)


def flat(rows, width):
    return pltpu.VMEM((rows * width, 256), BF)


def edges_call(own):
    return call(
        edges_kernel, "edges", [(32, HALO, 256), (32, HALO, 256), (DEEP, 32, 256)], [VMEM], [VMEM] * 3, [],
        EDGE_CELLS, (own,),
    )


def cut_call(north):
    return call(cut_kernel, "cut", [(DEEP, HALO, 256)] * 2, [VMEM], [VMEM] * 2, [], 0, (north,))


def first_call(*args):
    (x1,) = call(
        first_kernel, "first", [(30 * 24, 256)], [VMEM] * len(args), [VMEM],
        [taps(34, 24), flat(30, 24)], 720, args,
    )
    return x1


def second_call(*args):
    return call(
        second_kernel, "second", [(30 * 24, 256), (26 * 16, 256), (32 * 32, 128), ((32, 64), F32), ((DEEP, 64), F32)],
        [VMEM] * len(args), [VMEM] * 5,
        [taps(34, 16), flat(26, 16), pltpu.VMEM((26 * 16, 128), BF)], 416, args,
    )


def south_call(*args):
    return call(
        south_kernel, "south", [(8 * 56, 256), (16 * 48, 256), (18, 32, 256)], [VMEM] * len(args), [VMEM] * 3,
        [taps(34, 32), taps(34, 32), taps(34, 32), flat(30, 32), flat(26, 32), flat(30, 32),
         pltpu.VMEM((30 * 32, 128), BF), pltpu.VMEM((26 * 32, 128), BF)],
        2368, args,
    )


def fold_call(*args):
    return call(
        fold_kernel, "fold", [(14 * 24, 256), (14 * 16, 256), (14 * 32, 128), (14 * 32, 128)],
        [VMEM] * len(args), [VMEM] * 4,
        [taps(18, 24), taps(22, 16), flat(14, 24), pltpu.VMEM((14 * 24, 128), BF), pltpu.VMEM((14 * 16, 128), BF)],
        560, args,
    )


def north_call(*args):
    (out,) = call(
        north_kernel, "north", [(32, 32, 256)], [VMEM] * len(args), [HBM],
        [
            taps(18, 32), taps(22, 32), taps(30, 32), flat(14, 32), flat(14, 32), flat(14, 32),
            pltpu.VMEM((14, 32, 256), BF), pltpu.SemaphoreType.DMA((3,)),
        ],
        1344, args,
    )
    return out


def swap_inner(value):
    return lax.ppermute(value, "lon", [(i, i ^ 1) for i in range(lax.axis_size("lon"))])


def swap_outer(value, ring=1):
    count = lax.axis_size("lon") // ring
    return lax.ppermute(
        value, "lon", [(i, i // count * count + (((i + 1) ^ 1) - 1) % count) for i in range(ring * count)]
    )


def per_device(own, land_sea, w, up, down):
    count = lax.axis_size("lon")
    cols = own.shape[1]
    to_inner, to_outer, top = edges_call(own)
    inner = swap_inner(to_inner)
    outer = swap_outer(to_outer)
    weights = (w, up, down)
    x1_mid = first_call(own, *weights)
    top, x1_mid = lax.optimization_barrier((top, x1_mid))
    north = lax.ppermute(top, "lon", [(i, count - 1 - i) for i in range(count)])
    x1_mid, x2_mid, mask, land, land_north = second_call(x1_mid, land_sea, *weights)
    x1_tail, x2_tail, out_south = south_call(inner, own, outer, x1_mid, x2_mid, land, mask, *weights)
    north, x1_tail = lax.optimization_barrier((north, x1_tail))
    to_inner, to_outer = cut_call(north)
    north_inner = swap_inner(to_inner)
    north_outer = swap_outer(to_outer, 2)
    y1_mid, y2_mid, e1, e2 = fold_call(own, north, x1_tail, land, land_north, *weights)
    return north_call(
        inner, own, outer, north, north_inner, north_outer, x1_tail, x2_tail, out_south, y1_mid, y2_mid, e1, e2, mask, *weights
    )


def solution(mesh):
    in_specs = (P("parts", "lon", None), P(), P(), P(), P())
    out_specs = P("parts", "lon", None)
    return jax.shard_map(
        per_device, mesh=mesh, in_specs=in_specs, out_specs=out_specs, check_vma=False
    )
```

```python
import functools

import jax
import jax.numpy as jnp
import numpy as np
from jax import lax
from jax.experimental import pallas as pl
from jax.experimental.pallas import tpu as pltpu
from jax.sharding import PartitionSpec as P

BF = jnp.bfloat16
F32 = jnp.float32
HALO = 16
DEEP = 14
LIMIT = 20
EDGE_CELLS = 2048
RSQRT2 = np.float32(0.7071067811865476)


def conv_norm(layer, shifted, width, base, chunks, w_ref, nrm):
    dil = 2 ** (layer + 1)
    weight = w_ref[layer].reshape(-1, w_ref.shape[-1])
    at = 0
    for first, count, turned in chunks:
        taps = [(a, b) for a in range(3) for b in range(3)]
        if turned:
            taps = taps[::-1]
        size = count * width
        lhs = jnp.concatenate(
            [
                shifted[b, (first - base + (a - 1) * dil) * width : (first - base + (a - 1) * dil) * width + size]
                for a, b in taps
            ],
            axis=1,
        )
        conv = jnp.dot(lhs, weight, preferred_element_type=F32)
        mean = jnp.mean(conv, axis=-1, keepdims=True)
        centred = conv - mean
        var = jnp.mean(centred * centred, axis=-1, keepdims=True)
        nrm[at : at + size] = (centred * lax.rsqrt(var + 1e-05)).astype(BF)
        at += size


def mlp(layer, shifted, width, base, first, counts, up_ref, down_ref, mask_ref, nrm, store, mask_base=0):
    at = 0
    row = first
    for count in counts:
        size = count * width
        pre = jnp.dot(nrm[at : at + size], up_ref[layer], preferred_element_type=F32)
        hidden = (0.5 * pre * (1.0 + lax.erf(pre * RSQRT2))).astype(BF)
        branch = jnp.dot(hidden, down_ref[layer], preferred_element_type=F32)
        centre = shifted[1, (row - base) * width : (row - base) * width + size].astype(F32)
        mask = mask_ref[(row - mask_base) * width : (row - mask_base) * width + size].astype(F32)
        mask = jnp.concatenate([mask, mask], axis=1)
        store(row, count, (mask * (centre + branch)).astype(BF))
        at += size
        row += count


def spread(shifted, at, values, starts, size, dil):
    for b in range(3):
        for k, start in enumerate(starts):
            lo = start + (b - 1) * dil
            shifted[b, at + k * size : at + (k + 1) * size] = values[lo : lo + size]


def clear(shifted, size):
    for b in range(3):
        shifted[b, :size] = jnp.zeros((size, shifted.shape[-1]), BF)


def keep(ref, width, base):
    def store(row, count, value):
        ref[(row - base) * width : (row - base + count) * width] = value

    return store


def diagonal(turned, size=64):
    rows = lax.broadcasted_iota(jnp.int32, (size, size), 0)
    cols = lax.broadcasted_iota(jnp.int32, (size, size), 1)
    return rows + cols == size - 1 if turned else rows == cols


def spread_mask(land, first, count, turned):
    lines = jnp.where(diagonal(turned)[None], land[first : first + count][:, None, :], 0.0).astype(BF)
    cells = jnp.dot(lines.reshape(count * 64, 64), jnp.ones((64, 128), BF), preferred_element_type=F32)
    return cells.astype(BF).reshape(count, 64, 128)


def window(whole, first):
    total = whole.shape[1]
    source = lax.broadcasted_iota(jnp.int32, (total, 64), 0)
    target = lax.broadcasted_iota(jnp.int32, (total, 64), 1) + first
    target = jnp.where(target < 0, target + total, target)
    target = jnp.where(target >= total, target - total, target)
    pick = jnp.where(source == target, 1.0, 0.0).astype(BF)
    return jnp.dot(whole, pick, preferred_element_type=F32)


def halves(value, inner, outer):
    odd = lax.rem(lax.axis_index("lon"), 2) == 1
    for row in range(value.shape[0]):
        low, high = value[row, 0:HALO], value[row, 32 - HALO : 32]
        inner[row] = jnp.where(odd, low, high)
        outer[row] = jnp.where(odd, high, low)


def edges_kernel(own, inner, outer, top):
    halves(own, inner, outer)
    top[...] = own[32 - DEEP : 32]


def cut_kernel(north, inner, outer):
    halves(north, outer, inner)


def in_order(row, inner, outer):
    odd = lax.rem(lax.axis_index("lon"), 2) == 1
    return jnp.where(odd, inner[row], outer[row]), jnp.where(odd, outer[row], inner[row])


def wide(row, inner, own, outer):
    before, after = in_order(row, inner, outer)
    return jnp.concatenate([before, own[row], after], axis=0)


def first_kernel(own, land_sea, w, up, down, x1, mask, land, land_north, sh1, nrm, m1):
    me = lax.axis_index("lon")
    whole = land_sea[...].astype(F32).astype(BF)
    land[...] = window(whole, me * 32 - HALO)
    land_north[...] = window(whole, (lax.axis_size("lon") - 1 - me) * 32 - HALO)[32 - DEEP :]
    cells = spread_mask(land, 0, 32, False)
    mask[...] = cells[:, 16:48].reshape(32 * 32, 128)
    m1[...] = cells[:30, 20:44].reshape(30 * 24, 128)
    clear(sh1, 2 * 24)
    for row in range(32):
        spread(sh1, (row + 2) * 24, own[row], [4], 24, 2)
    conv_norm(0, sh1, 24, -2, [(0, 8, False), (8, 8, False), (16, 8, False), (24, 6, False)], w, nrm)
    mlp(0, sh1, 24, -2, 0, [10, 10, 10], up, down, m1, nrm, keep(x1, 24, 0))


def second_kernel(x1, mask, w, up, down, x2, sh2, nrm, m2):
    for row in range(26):
        m2[row * 16 : (row + 1) * 16] = mask[row * 32 + 8 : row * 32 + 24]
    clear(sh2, 4 * 16)
    for row in range(30):
        spread(sh2, (row + 4) * 16, x1[row * 24 : (row + 1) * 24], [4], 16, 4)
    conv_norm(1, sh2, 16, -4, [(0, 13, False), (13, 13, False)], w, nrm)
    mlp(1, sh2, 16, -4, 0, [13, 13], up, down, m2, nrm, keep(x2, 16, 0))


def south_kernel(
    inner, own, outer, x1_mid, x2_mid, land, mask, w, up, down,
    x1_tail, x2_tail, out, sh1, sh2, sh3, x1, x2, nrm, e1, e2,
):
    clear(sh1, 2 * 32)
    clear(sh2, 4 * 32)
    clear(sh3, 8 * 32)
    for row in range(32):
        spread(sh1, (row + 2) * 32, wide(row, inner, own, outer), [4, 44], 16, 2)
    cells = spread_mask(land, 0, 30, False)
    e1[...] = jnp.concatenate([cells[:, 4:20], cells[:, 44:60]], axis=1).reshape(30 * 32, 128)
    e2[...] = jnp.concatenate([cells[:26, 8:24], cells[:26, 40:56]], axis=1).reshape(26 * 32, 128)
    conv_norm(0, sh1, 32, -2, [(0, 8, False), (8, 8, False), (16, 7, False), (23, 7, False)], w, nrm)
    mlp(0, sh1, 32, -2, 0, [15, 15], up, down, e1, nrm, keep(x1, 32, 0))

    def row1(row):
        at = row * 32
        return jnp.concatenate([x1[at : at + 16], x1_mid[row * 24 : (row + 1) * 24], x1[at + 16 : at + 32]], axis=0)

    for row in range(30):
        values = row1(row)
        if row >= 22:
            x1_tail[(row - 22) * 56 : (row - 21) * 56] = values
        spread(sh2, (row + 4) * 32, values, [4, 36], 16, 4)
    conv_norm(1, sh2, 32, -4, [(0, 8, False), (8, 6, False), (14, 6, False), (20, 6, False)], w, nrm)
    mlp(1, sh2, 32, -4, 0, [13, 13], up, down, e2, nrm, keep(x2, 32, 0))
    for row in range(26):
        at = row * 32
        values = jnp.concatenate([x2[at : at + 16], x2_mid[row * 16 : (row + 1) * 16], x2[at + 16 : at + 32]], axis=0)
        if row >= 10:
            x2_tail[(row - 10) * 48 : (row - 9) * 48] = values
        spread(sh3, (row + 8) * 32, values, [8], 32, 8)
    conv_norm(2, sh3, 32, -8, [(0, 6, False), (6, 6, False), (12, 6, False)], w, nrm)

    def store3(row, count, value):
        out[row : row + count] = value.reshape(count, 32, 256)

    mlp(2, sh3, 32, -8, 0, [12, 6], up, down, mask, nrm, store3)


def strips(cells, left, right):
    rows = cells.shape[0]
    return jnp.concatenate([cells[:, left : left + 16], cells[:, right : right + 16]], axis=1).reshape(rows * 32, 128)


def fold_kernel(own, north, x1_tail, land, land_north, w, up, down, x1, x2, e1, e2, sh1, sh2, nrm, m1, m2):
    near = spread_mask(land, 26, 6, False)
    far = spread_mask(land_north, 0, DEEP, True)
    cells = jnp.concatenate([near] + [far[45 - row : 46 - row] for row in range(32, 44)], axis=0)
    m1[...] = cells[4:, 20:44].reshape(14 * 24, 128)
    m2[...] = cells[:14, 24:40].reshape(14 * 16, 128)
    e1[...] = strips(cells[4:], 4, 44)
    e2[...] = strips(cells[:14], 8, 40)
    turn = jnp.where(diagonal(True, 32), 1.0, 0.0).astype(BF)
    for row in range(18):
        if row < 4:
            line = own[28 + row]
        else:
            line = jnp.dot(turn, north[17 - row], preferred_element_type=F32).astype(BF)
        spread(sh1, row * 24, line, [4], 24, 2)
    conv_norm(0, sh1, 24, 28, [(30, 2, False), (32, 6, True), (38, 6, True)], w, nrm)
    mlp(0, sh1, 24, 28, 30, [8, 6], up, down, m1, nrm, keep(x1, 24, 30), 30)
    for row in range(8):
        spread(sh2, row * 16, x1_tail[row * 56 : (row + 1) * 56], [20], 16, 4)
    for row in range(14):
        spread(sh2, (row + 8) * 16, x1[row * 24 : (row + 1) * 24], [4], 16, 4)
    conv_norm(1, sh2, 16, 22, [(26, 6, False), (32, 8, True)], w, nrm)
    mlp(1, sh2, 16, 22, 26, [7, 7], up, down, m2, nrm, keep(x2, 16, 26), 26)


def north_kernel(
    inner, own, outer, north, north_inner, north_outer, x1_tail, x2_tail, out_south, x1_mid, x2_mid,
    e1, e2, mask, w, up, down, out, sh1, sh2, sh3, x1, x2, nrm, last, sems,
):
    first = pltpu.make_async_copy(out_south, out.at[0:18], sems.at[0])
    first.start()
    half = lax.axis_size("lon") // 2
    place = lax.rem(lax.axis_index("lon"), half)
    turn = jnp.where(diagonal(True), 1.0, 0.0).astype(BF)
    for row in range(4):
        spread(sh1, row * 32, wide(28 + row, inner, own, outer), [4, 44], 16, 2)
    for row in range(14):
        at = 13 - row
        after, before = in_order(at, north_inner, north_outer)
        after = jnp.where(place == 0, own[18 + at, 0:HALO], after)
        before = jnp.where(place == half - 1, own[18 + at, 32 - HALO : 32], before)
        source = jnp.concatenate([before, north[at], after], axis=0)
        turned = jnp.dot(turn, source, preferred_element_type=F32).astype(BF)
        spread(sh1, (row + 4) * 32, turned, [4, 44], 16, 2)
    conv_norm(0, sh1, 32, 28, [(30, 2, False), (32, 6, True), (38, 6, True)], w, nrm)
    mlp(0, sh1, 32, 28, 30, [7, 7], up, down, e1, nrm, keep(x1, 32, 30), 30)
    for row in range(8):
        spread(sh2, row * 32, x1_tail[row * 56 : (row + 1) * 56], [4, 36], 16, 4)
    for row in range(14):
        at = row * 32
        values = jnp.concatenate([x1[at : at + 16], x1_mid[row * 24 : (row + 1) * 24], x1[at + 16 : at + 32]], axis=0)
        spread(sh2, (row + 8) * 32, values, [4, 36], 16, 4)
    conv_norm(1, sh2, 32, 22, [(26, 6, False), (32, 4, True), (36, 4, True)], w, nrm)
    mlp(1, sh2, 32, 22, 26, [5, 5, 4], up, down, e2, nrm, keep(x2, 32, 26), 26)
    for row in range(16):
        spread(sh3, row * 32, x2_tail[row * 48 : (row + 1) * 48], [8], 32, 8)
    for row in range(14):
        at = row * 32
        values = jnp.concatenate([x2[at : at + 16], x2_mid[row * 16 : (row + 1) * 16], x2[at + 16 : at + 32]], axis=0)
        spread(sh3, (row + 16) * 32, values, [8], 32, 8)
    conv_norm(2, sh3, 32, 10, [(18, 7, False), (25, 7, False)], w, nrm)

    copies = [first]

    def store3(row, count, value):
        last[row - 18 : row - 18 + count] = value.reshape(count, 32, 256)
        here = pltpu.make_async_copy(
            last.at[row - 18 : row - 18 + count], out.at[row : row + count], sems.at[len(copies)]
        )
        here.start()
        copies.append(here)

    mlp(2, sh3, 32, 10, 18, [8, 6], up, down, mask, nrm, store3)
    for copy in copies:
        copy.wait()


def cost(cells):
    return pl.CostEstimate(
        flops=2 * cells * (9 * 256 * 256 + 2 * 256 * 1024), bytes_accessed=2**20, transcendentals=cells * 1024
    )


VMEM = pl.BlockSpec(memory_space=pltpu.VMEM)
HBM = pl.BlockSpec(memory_space=pltpu.HBM)


def call(kernel, name, outs, in_specs, out_specs, scratch, cells, args, limit=LIMIT):
    return pl.pallas_call(
        kernel,
        name=name,
        out_shape=tuple(jax.ShapeDtypeStruct(*(out if isinstance(out[0], tuple) else (out, BF))) for out in outs),
        in_specs=in_specs,
        out_specs=tuple(out_specs),
        scratch_shapes=scratch,
        compiler_params=pltpu.CompilerParams(vmem_limit_bytes=limit * 2**20),
        cost_estimate=cost(cells),
    )(*args)


def taps(rows, width):
    return pltpu.VMEM((3, rows * width, 256), BF)


def flat(rows, width):
    return pltpu.VMEM((rows * width, 256), BF)


def edges_call(own):
    return call(
        edges_kernel, "edges", [(32, HALO, 256), (32, HALO, 256), (DEEP, 32, 256)], [VMEM], [VMEM] * 3, [],
        EDGE_CELLS, (own,),
    )


def cut_call(north):
    return call(cut_kernel, "cut", [(DEEP, HALO, 256)] * 2, [VMEM], [VMEM] * 2, [], 0, (north,))


def first_call(*args):
    return call(
        first_kernel, "first", [(30 * 24, 256), (32 * 32, 128), ((32, 64), F32), ((DEEP, 64), F32)],
        [VMEM] * len(args), [VMEM] * 4,
        [taps(34, 24), flat(30, 24), pltpu.VMEM((30 * 24, 128), BF)], 720, args,
    )


def second_call(*args):
    (x2,) = call(
        second_kernel, "second", [(26 * 16, 256)], [VMEM] * len(args), [VMEM],
        [taps(34, 16), flat(26, 16), pltpu.VMEM((26 * 16, 128), BF)], 416, args,
    )
    return x2


def south_call(*args):
    return call(
        south_kernel, "south", [(8 * 56, 256), (16 * 48, 256), (18, 32, 256)], [VMEM] * len(args), [VMEM] * 3,
        [taps(34, 32), taps(34, 32), taps(34, 32), flat(30, 32), flat(26, 32), flat(30, 32),
         pltpu.VMEM((30 * 32, 128), BF), pltpu.VMEM((26 * 32, 128), BF)],
        2368, args,
    )


def fold_call(*args):
    return call(
        fold_kernel, "fold", [(14 * 24, 256), (14 * 16, 256), (14 * 32, 128), (14 * 32, 128)],
        [VMEM] * len(args), [VMEM] * 4,
        [taps(18, 24), taps(22, 16), flat(14, 24), pltpu.VMEM((14 * 24, 128), BF), pltpu.VMEM((14 * 16, 128), BF)],
        560, args,
    )


def north_call(*args):
    (out,) = call(
        north_kernel, "north", [(32, 32, 256)], [VMEM] * len(args), [HBM],
        [
            taps(18, 32), taps(22, 32), taps(30, 32), flat(14, 32), flat(14, 32), flat(14, 32),
            pltpu.VMEM((14, 32, 256), BF), pltpu.SemaphoreType.DMA((3,)),
        ],
        1344, args,
    )
    return out


def swap_inner(value):
    return lax.ppermute(value, "lon", [(i, i ^ 1) for i in range(lax.axis_size("lon"))])


def swap_outer(value, ring=1):
    count = lax.axis_size("lon") // ring
    return lax.ppermute(
        value, "lon", [(i, i // count * count + (((i + 1) ^ 1) - 1) % count) for i in range(ring * count)]
    )


def per_device(own, land_sea, w, up, down):
    count = lax.axis_size("lon")
    cols = own.shape[1]
    to_inner, to_outer, top = edges_call(own)
    inner = swap_inner(to_inner)
    outer = swap_outer(to_outer)
    weights = (w, up, down)
    x1_mid, mask, land, land_north = first_call(own, land_sea, *weights)
    top, x1_mid = lax.optimization_barrier((top, x1_mid))
    north = lax.ppermute(top, "lon", [(i, count - 1 - i) for i in range(count)])
    x2_mid = second_call(x1_mid, mask, *weights)
    x1_tail, x2_tail, out_south = south_call(inner, own, outer, x1_mid, x2_mid, land, mask, *weights)
    north, x1_tail = lax.optimization_barrier((north, x1_tail))
    to_inner, to_outer = cut_call(north)
    north_inner = swap_inner(to_inner)
    north_outer = swap_outer(to_outer, 2)
    y1_mid, y2_mid, e1, e2 = fold_call(own, north, x1_tail, land, land_north, *weights)
    return north_call(
        inner, own, outer, north, north_inner, north_outer, x1_tail, x2_tail, out_south, y1_mid, y2_mid, e1, e2, mask, *weights
    )


def solution(mesh):
    in_specs = (P("parts", "lon", None), P(), P(), P(), P())
    out_specs = P("parts", "lon", None)
    return jax.shard_map(
        per_device, mesh=mesh, in_specs=in_specs, out_specs=out_specs, check_vma=False
    )
```
